128 devices in a mesh: ctx: 32 (over x, y_hi, z), ch: 4 (over y_lo, core).
Axes of the slice: x: 4, y: 4 (y_hi: 2, y_lo: 2; y = y_hi * 2 + y_lo), z: 4, core: 2. Of those that a mesh axis runs over, the one named last changes fastest.
Arguments:
- branches: bfloat16 [3, 256, 65536], P(None, 'ch', 'ctx'), may hold values from -6 to 6
- short_taps: float32 [3, 256, 7], P(None, 'ch'), may hold values from -2 to 2
- long_filter: float32 [64, 65536], P('ch', 'ctx'), may hold values from -1.5 to 1.5
- skip_gain: float32 [256], P('ch'), may hold values from 0.5 to 1.5
Outputs:
- mixed: bfloat16 [256, 65536], P('ch', 'ctx')
The draws below stay inside these ranges and needn't reach their ends.
All inputs are finite; a program needn't handle non-finite values.
Results may differ from the reference program's by a relative error of at most 0.0095.
Values may be sent and summed in bfloat16 or wider, within the bound.
No kernel may reach another device: no remote copies, remote signals or barrier semaphores. Data moves between devices by JAX's collectives and lax.ppermute only.
A program may use at most 128 MiB of HBM per device.

```python
import jax
import jax.numpy as jnp

CHANNELS_PER_UNIT = 64
TOK_DEV = 2048
SHORT = 7
SEQUENCE_TOKENS = 65536
CHANNELS = 256
N_CH = 4


def draw_long_filter(key, part):
    key = jax.random.fold_in(key, 11)
    random_keys = jax.random.split(key, 7)
    echo_keys = jax.random.split(random_keys[6], 3)
    noise = jnp.clip(jax.random.normal(random_keys[0], (CHANNELS_PER_UNIT, SEQUENCE_TOKENS), jnp.float32), -4.0, 4.0)
    echo_noise = jnp.clip(jax.random.normal(echo_keys[0], (CHANNELS_PER_UNIT, SEQUENCE_TOKENS), jnp.float32), -4.0, 4.0)
    share = 0.5
    slow = jax.random.uniform(random_keys[1], (CHANNELS_PER_UNIT, 1), jnp.float32) < share
    slow_rate = jax.random.uniform(random_keys[2], (CHANNELS_PER_UNIT, 1), jnp.float32, 0.2, 2.0) / SEQUENCE_TOKENS
    fast_rate = 1.0 / jax.random.uniform(random_keys[3], (CHANNELS_PER_UNIT, 1), jnp.float32, 20.0, 60.0)
    rate = jnp.where(slow, slow_rate, fast_rate)
    token_offsets = jnp.arange(SEQUENCE_TOKENS, dtype=jnp.int32).astype(jnp.float32)[None, :]
    decay_profile = jnp.exp(-rate * token_offsets)
    pulse_position = jax.random.randint(random_keys[4], (CHANNELS_PER_UNIT, 3), 0, SEQUENCE_TOKENS).astype(jnp.float32)
    pulse_mask = jax.random.uniform(random_keys[5], (CHANNELS_PER_UNIT, 3), jnp.float32, 0.5, 0.8)
    for pulse_values in range(3):
        decay_profile = decay_profile * jnp.where(token_offsets >= pulse_position[:, pulse_values:pulse_values + 1], pulse_mask[:, pulse_values:pulse_values + 1], 1.0)
    scaling = jnp.sqrt(2.0 * rate / (1.0 - jnp.exp(-2.0 * rate * SEQUENCE_TOKENS)))
    head = noise * decay_profile * scaling
    echo_rate = jax.random.uniform(echo_keys[1], (CHANNELS_PER_UNIT, 1), jnp.float32, 0.2, 2.0) / SEQUENCE_TOKENS
    echo_start = jax.random.randint(echo_keys[2], (CHANNELS_PER_UNIT, 1), 2 * TOK_DEV, SEQUENCE_TOKENS // 2 + 1).astype(jnp.float32)
    echo_length = SEQUENCE_TOKENS - echo_start
    echo_scale = jnp.sqrt(2.0 * echo_rate / (1.0 - jnp.exp(-2.0 * echo_rate * echo_length)))
    echo_offset = jnp.maximum(token_offsets - echo_start, 0.0)
    echo = jnp.where(token_offsets >= echo_start, 0.6 * echo_noise * jnp.exp(-echo_rate * echo_offset) * echo_scale, 0.0)
    echo = jnp.where(slow, 0.0, echo)
    return jnp.clip(head + echo, -1.5, 1.5)


def level_of(stream_key, shape, cuts, low, high):
    gain, own = 1.0, jax.random.fold_in(stream_key, 6)
    for position, blocks in cuts:
        draws = jnp.exp(jax.random.uniform(jax.random.fold_in(own, position), (blocks,), jnp.float32, low / len(cuts), high / len(cuts)))
        gain = gain * jnp.repeat(draws, shape[position] // blocks).reshape([-1 if axis == position else 1 for axis in range(len(shape))])
    return gain


def normal_values(own_key, extent, scale, reach, cuts=(), kind=jnp.bfloat16):
    array = scale * jax.random.normal(own_key, extent, jnp.float32)
    if cuts:
        array = array * level_of(own_key, extent, cuts, -0.22, 0.18)
    return jnp.clip(array, -reach, reach).astype(kind)


def setup_inputs(seed: int = 0) -> dict:
    streams_of = jax.random.split(jax.random.key(seed), 5)
    branches = normal_values(streams_of[0], (3, CHANNELS, SEQUENCE_TOKENS), 1.0, 6.0, ((1, 4), (2, 32)))
    short_taps = normal_values(streams_of[1], (3, CHANNELS, SHORT), SHORT ** -0.5, 2.0, ((1, 4),), jnp.float32)
    long_filter = draw_long_filter(jax.random.fold_in(streams_of[4], 71), 0)
    skip_gain = jnp.clip(0.5 + 1.0 * jax.random.uniform(streams_of[3], (CHANNELS,), jnp.float32) ** level_of(streams_of[3], (CHANNELS,), ((0, 4),), -0.2, 0.2), 0.5, 1.5)
    return dict(branches=branches, short_taps=short_taps, long_filter=long_filter, skip_gain=skip_gain)


def reference(branches, short_taps, long_filter, skip_gain):
    length = branches.shape[-1]
    signal = branches.astype(jnp.float32)
    padded = jnp.pad(signal, ((0, 0), (0, 0), (SHORT - 1, 0)))
    short = sum(short_taps[:, :, tap:tap + 1] * padded[:, :, SHORT - 1 - tap:SHORT - 1 - tap + length] for tap in range(SHORT))
    query = short[0]
    gated = short[1] * short[2]
    total = 2 * length
    gated_spec = jnp.fft.rfft(gated, n=total, axis=-1)
    filter_spec = jnp.tile(jnp.fft.rfft(long_filter, n=total, axis=-1), (N_CH, 1))
    conv = jnp.fft.irfft(gated_spec * filter_spec, n=total, axis=-1)[:, :length]
    return (query * (conv + skip_gain[:, None] * gated)).astype(jnp.bfloat16)
```

```python
import functools

import jax
import jax.numpy as jnp
from jax import lax
from jax.experimental import pallas as pl
from jax.experimental.pallas import tpu as pltpu
from jax.sharding import PartitionSpec as P

f32, bf16 = jnp.float32, jnp.bfloat16
LANES = 128
TAPS = 7
CHANNELS = 64
TOKENS = 2048
BLOCKS = TOKENS // LANES
PARTS = 32
OWN = CHANNELS // PARTS
ROWS = PARTS * BLOCKS
HALF = OWN * BLOCKS
GROUP = 8
VMEM = pl.BlockSpec(memory_space=pltpu.VMEM)


def short_kernel(branch_ref, tail_ref, taps_ref, skip_ref, filter_ref, send_ref, query_ref, direct_ref, rows_ref):
    send_ref[:, HALF:, :] = filter_ref[...]
    step = 16
    for base in range(0, CHANNELS, step):
        rows = slice(base, base + step)
        short = []
        for branch in range(3):
            own = branch_ref[branch, rows, :].astype(f32)
            extended = jnp.concatenate([tail_ref[branch, rows, :].astype(f32), own], axis=1)
            taps = taps_ref[branch, rows, :]
            total = taps[:, 0:1] * own
            for tap in range(1, TAPS):
                total += taps[:, tap : tap + 1] * extended[:, LANES - tap : LANES - tap + TOKENS]
            short.append(total)
        gated = short[1] * short[2]
        query_ref[rows, :] = short[0]
        direct_ref[rows, :] = short[0] * (skip_ref[rows, :] * gated)
        for block in range(BLOCKS):
            rows_ref[pl.ds(base * BLOCKS + block, step, stride=BLOCKS), :] = gated[
                :, block * LANES : (block + 1) * LANES
            ]
    send_ref[:, :HALF, :] = rows_ref[...].reshape(PARTS, HALF, LANES).astype(bf16)


def conv_kernel(data_ref, out_ref, signal_ref, taps_ref, left_ref, right_ref, sum_ref):
    shift = 2 * GROUP
    row = lax.broadcasted_iota(jnp.int32, (LANES, LANES), 0)
    lane = lax.broadcasted_iota(jnp.int32, (LANES, LANES), 1)
    above = lane >= row
    for own in range(OWN):
        begin = own * BLOCKS
        signal_ref[:shift, :] = jnp.zeros((shift, LANES), f32)
        signal_ref[shift:, :] = data_ref[:, begin : begin + BLOCKS, :].reshape(ROWS, LANES).astype(f32)
        taps_ref[...] = data_ref[:, HALF + begin : HALF + begin + BLOCKS, :].reshape(ROWS, LANES).astype(f32)
        for lag in range(GROUP):
            left_ref[:, lag * LANES : (lag + 1) * LANES] = signal_ref[
                shift - 2 * lag : shift - 2 * lag + ROWS, :
            ].astype(bf16)
        previous = jnp.zeros((LANES, LANES), f32)
        for group in range(ROWS // shift):
            slot = group % 2
            for lag in range(shift):
                block = group * shift + lag
                spread = jnp.broadcast_to(taps_ref[block : block + 1, :], (LANES, LANES))
                current = pltpu.roll(spread, 0, 1, stride=1, stride_axis=0)
                right_ref[
                    slot, (lag // 2) * LANES : (lag // 2 + 1) * LANES, (lag % 2) * LANES : (lag % 2 + 1) * LANES
                ] = jnp.where(above, current, previous).astype(bf16)
                previous = current
            product = jnp.dot(
                left_ref[: ROWS - shift * group, :], right_ref[slot], preferred_element_type=f32
            )
            if group == 0:
                sum_ref[shift:, :] = product
            else:
                sum_ref[shift + shift * group :, :] += product
        sum_ref[:shift, :] = jnp.zeros((shift, 2 * LANES), f32)
        result = sum_ref[shift:, :LANES] + sum_ref[shift - 1 : shift - 1 + ROWS, LANES:]
        out_ref[:, begin : begin + BLOCKS, :] = result.astype(bf16).reshape(PARTS, BLOCKS, LANES)


def mix_kernel(conv_ref, query_ref, direct_ref, out_ref, rows_ref):
    rows_ref[...] = conv_ref[...].reshape(CHANNELS * BLOCKS, LANES).astype(f32)
    for block in range(BLOCKS):
        columns = slice(block * LANES, (block + 1) * LANES)
        conv = rows_ref[pl.ds(block, CHANNELS, stride=BLOCKS), :]
        out_ref[:, columns] = (query_ref[:, columns] * conv + direct_ref[:, columns]).astype(bf16)


def on_device(branches, short_taps, long_filter, skip_gain):
    tails = lax.ppermute(branches[:, :, TOKENS - LANES :], "ctx", [(i, i + 1) for i in range(PARTS - 1)])
    filters = long_filter.reshape(long_filter.shape[0], BLOCKS, LANES).astype(bf16)
    filters = lax.all_gather(filters, "ch", axis=0, tiled=True).reshape(PARTS, HALF, LANES)
    send, query, direct = pl.pallas_call(
        short_kernel,
        out_shape=[
            jax.ShapeDtypeStruct((PARTS, 2 * HALF, LANES), bf16),
            jax.ShapeDtypeStruct((CHANNELS, TOKENS), f32),
            jax.ShapeDtypeStruct((CHANNELS, TOKENS), f32),
        ],
        in_specs=[VMEM] * 5,
        out_specs=[VMEM] * 3,
        scratch_shapes=[pltpu.VMEM((CHANNELS * BLOCKS, LANES), f32)],
        compiler_params=pltpu.CompilerParams(vmem_limit_bytes=32 * 2**20),
    )(branches, tails, short_taps, skip_gain[:, None], filters)
    data = lax.all_to_all(send, "ctx", 0, 0, tiled=True)
    conv = pl.pallas_call(
        conv_kernel,
        out_shape=jax.ShapeDtypeStruct((PARTS, HALF, LANES), bf16),
        in_specs=[VMEM],
        out_specs=VMEM,
        scratch_shapes=[
            pltpu.VMEM((2 * GROUP + ROWS, LANES), f32),
            pltpu.VMEM((ROWS, LANES), f32),
            pltpu.VMEM((ROWS, GROUP * LANES), bf16),
            pltpu.VMEM((2, GROUP * LANES, 2 * LANES), bf16),
            pltpu.VMEM((2 * GROUP + ROWS, 2 * LANES), f32),
        ],
        compiler_params=pltpu.CompilerParams(vmem_limit_bytes=32 * 2**20),
    )(data)
    conv = lax.all_to_all(conv, "ctx", 0, 0, tiled=True)
    return pl.pallas_call(
        mix_kernel,
        out_shape=jax.ShapeDtypeStruct((CHANNELS, TOKENS), bf16),
        in_specs=[VMEM] * 3,
        out_specs=VMEM,
        scratch_shapes=[pltpu.VMEM((CHANNELS * BLOCKS, LANES), f32)],
        compiler_params=pltpu.CompilerParams(vmem_limit_bytes=32 * 2**20),
    )(conv, query, direct)


def solution(mesh):
    placed = (P(None, "ch", "ctx"), P(None, "ch", None), P("ch", "ctx"), P("ch"))
    return jax.shard_map(
        on_device, mesh=mesh, in_specs=placed, out_specs=P("ch", "ctx"), check_vma=False
    )
```

```python
import jax
import jax.numpy as jnp
from jax import lax
from jax.experimental import pallas as pl
from jax.experimental.pallas import tpu as pltpu
from jax.sharding import PartitionSpec as P

f32, bf16 = jnp.float32, jnp.bfloat16
LANES = 128
TAPS = 7
CHANNELS = 64
TOKENS = 2048
BLOCKS = TOKENS // LANES
PARTS = 32
FILTERS = 16
OWN = CHANNELS // PARTS
ROWS = PARTS * BLOCKS
HALF = OWN * BLOCKS
GROUP = 8
WIDTH = LANES // 2
VMEM = pl.BlockSpec(memory_space=pltpu.VMEM)


def spread(taps_ref, branch, rows, count):
    taps = taps_ref[branch, rows, :]
    return [jnp.broadcast_to(taps[:, tap : tap + 1], (count, LANES)) for tap in range(TAPS)]


def short_kernel(branch_ref, taps_ref, skip_ref, rows_ref, query_ref, direct_ref):
    step = 16
    lane = lax.broadcasted_iota(jnp.int32, (step, LANES), 1)

    def body(index, carry):
        rows = pl.ds(pl.multiple_of(index * step, step), step)

        def filtered(branch):
            taps = spread(taps_ref, branch, rows, step)
            before = [jnp.zeros((step, LANES), f32)] * (TAPS - 1)
            for block in range(BLOCKS):
                own = branch_ref[branch, rows, block * LANES : (block + 1) * LANES].astype(f32)
                total = taps[0] * own
                for tap in range(1, TAPS):
                    turned = pltpu.roll(own, tap, 1)
                    total += taps[tap] * jnp.where(lane < tap, before[tap - 1], turned)
                    before[tap - 1] = turned
                yield total

        skip = jnp.broadcast_to(skip_ref[rows, :], (step, LANES))
        for block, total in enumerate(filtered(1)):
            direct_ref[rows, block * LANES : (block + 1) * LANES] = total
        for block, total in enumerate(filtered(2)):
            columns = slice(block * LANES, (block + 1) * LANES)
            gated = direct_ref[rows, columns] * total
            direct_ref[rows, columns] = skip * gated
            rows_ref[pl.ds(index * (step * BLOCKS) + block, step, stride=BLOCKS), :] = gated
        for block, total in enumerate(filtered(0)):
            columns = slice(block * LANES, (block + 1) * LANES)
            query_ref[rows, columns] = total
            direct_ref[rows, columns] = total * direct_ref[rows, columns]
        return carry

    lax.fori_loop(0, CHANNELS // step, body, 0)


def pack_kernel(
    branch_ref, tail_ref, taps_ref, skip_ref, rows_ref, own_ref, one_ref, two_ref, three_ref,
    send_ref, query_ref, direct_ref, work_ref,
):
    here = lax.axis_index("ch")
    owned = FILTERS // OWN
    for apart, taps_from in enumerate((own_ref, one_ref, two_ref, three_ref)):
        for block in range(BLOCKS):
            work_ref[pl.ds(block, FILTERS, stride=BLOCKS), :] = taps_from[:, block * LANES : (block + 1) * LANES]
        begin = pl.multiple_of((here ^ apart) * owned, owned)
        taps = work_ref[: FILTERS * BLOCKS, :].astype(bf16)
        send_ref[pl.ds(begin, owned), HALF:, :] = taps.reshape(owned, HALF, LANES)
    lane = lax.broadcasted_iota(jnp.int32, (CHANNELS, LANES), 1)
    short = []
    for branch in range(3):
        taps = spread(taps_ref, branch, slice(None), CHANNELS)
        before = tail_ref[branch].astype(f32)
        own = branch_ref[branch].astype(f32)
        total = taps[0] * own
        for tap in range(1, TAPS):
            total += taps[tap] * jnp.where(lane < tap, pltpu.roll(before, tap, 1), pltpu.roll(own, tap, 1))
        short.append(total)
    gated = short[1] * short[2]
    query_ref[...] = short[0]
    direct_ref[...] = short[0] * (skip_ref[...] * gated)
    work_ref[...] = rows_ref[...]
    work_ref[pl.ds(0, CHANNELS, stride=BLOCKS), :] = gated
    send_ref[:, :HALF, :] = work_ref[...].reshape(PARTS, HALF, LANES).astype(bf16)


def conv_kernel(data_ref, out_ref, signal_ref, taps_ref, left_ref, even_ref, odd_ref, sum_ref):
    shift = 2 * GROUP
    groups = ROWS // shift
    row = lax.broadcasted_iota(jnp.int32, (WIDTH, LANES), 0)
    lane = lax.broadcasted_iota(jnp.int32, (WIDTH, LANES), 1)
    above = lane >= row
    low = lax.broadcasted_iota(jnp.int32, (ROWS, LANES), 1) < WIDTH
    right = (even_ref, odd_ref)
    previous = jnp.zeros((WIDTH, LANES), f32)

    def load(own):
        begin = own * BLOCKS
        signal_ref[:shift, :] = jnp.zeros((shift, LANES), f32)
        signal_ref[shift:, :] = data_ref[:, begin : begin + BLOCKS, :].reshape(ROWS, LANES).astype(f32)
        taps = data_ref[:, HALF + begin : HALF + begin + BLOCKS, :]
        taps_ref[own] = taps.reshape(ROWS, LANES).astype(f32)
        for lag in range(0, GROUP, 2):
            near = signal_ref[shift - 2 * lag : shift - 2 * lag + ROWS, :]
            far = signal_ref[shift - 2 * lag - 2 : shift - 2 * lag - 2 + ROWS, :]
            columns = slice(lag * WIDTH, (lag + 2) * WIDTH)
            left_ref[own, 0, :, columns] = jnp.where(low, near, pltpu.roll(far, WIDTH, 1)).astype(bf16)
            left_ref[own, 1, :, columns] = jnp.where(low, pltpu.roll(near, WIDTH, 1), far).astype(bf16)

    def toeplitz(step, lag, previous):
        own, group = divmod(step, groups)
        block = group * shift + lag
        if block == 0:
            previous = jnp.zeros((WIDTH, LANES), f32)
        current = jnp.broadcast_to(taps_ref[own, block : block + 1, :], (WIDTH, LANES))
        current = pltpu.roll(current, 0, 1, stride=1, stride_axis=0)
        right[step % 2][
            (lag // 2) * WIDTH : (lag // 2 + 1) * WIDTH, (lag % 2) * LANES : (lag % 2 + 1) * LANES
        ] = jnp.where(above, current, previous).astype(bf16)
        return current

    def finish(own):
        sums = sum_ref.at[own]
        for half in range(2):
            sums[half, :shift, :] = jnp.zeros((shift, 2 * LANES), f32)

        def gather(half, back):
            here, there = shift - back, shift - back - 1
            return sums[half, here : here + ROWS, :LANES] + sums[half, there : there + ROWS, LANES:]

        turned = jnp.where(low, pltpu.roll(gather(1, 1), WIDTH, 1), pltpu.roll(gather(1, 0), WIDTH, 1))
        result = gather(0, 0) + turned
        out_ref[:, own * BLOCKS : (own + 1) * BLOCKS, :] = result.astype(bf16).reshape(PARTS, BLOCKS, LANES)

    for own in range(OWN):
        load(own)
    for lag in range(shift):
        previous = toeplitz(0, lag, previous)
    steps = OWN * groups
    for step in range(steps):
        own, group = divmod(step, groups)
        for half in range(2):
            if step + 1 < steps:
                for lag in range(half * GROUP, (half + 1) * GROUP):
                    previous = toeplitz(step + 1, lag, previous)
            product = jnp.dot(
                left_ref[own, half, : ROWS - shift * group, :], right[step % 2][...], preferred_element_type=f32
            )
            if group == 0:
                sum_ref[own, half, shift:, :] = product
            else:
                sum_ref[own, half, shift + shift * group :, :] += product
        if group == groups - 1:
            finish(own)


def mix_kernel(conv_ref, query_ref, direct_ref, first_query_ref, first_direct_ref, out_ref, rows_ref):
    rows_ref[...] = conv_ref[...].reshape(CHANNELS * BLOCKS, LANES).astype(f32)
    for block in range(BLOCKS):
        columns = slice(block * LANES, (block + 1) * LANES)
        conv = rows_ref[pl.ds(block, CHANNELS, stride=BLOCKS), :]
        query = query_ref[:, columns] if block else first_query_ref[...]
        direct = direct_ref[:, columns] if block else first_direct_ref[...]
        out_ref[:, columns] = (query * conv + direct).astype(bf16)


def whole(*shape):
    return pl.BlockSpec(shape, lambda i: (0,) * len(shape))


def on_device(branches, short_taps, long_filter, skip_gain):
    filters = [long_filter] + [
        lax.ppermute(long_filter, "ch", [(i, i ^ apart) for i in range(4)]) for apart in (1, 2, 3)
    ]
    tails = lax.ppermute(branches[:, :, TOKENS - LANES :], "ctx", [(i, i + 1) for i in range(PARTS - 1)])
    skip = skip_gain[:, None]
    rows, query, direct = pl.pallas_call(
        short_kernel,
        out_shape=[
            jax.ShapeDtypeStruct((CHANNELS * BLOCKS, LANES), f32),
            jax.ShapeDtypeStruct((CHANNELS, TOKENS), f32),
            jax.ShapeDtypeStruct((CHANNELS, TOKENS), f32),
        ],
        in_specs=[VMEM] * 3,
        out_specs=[VMEM] * 3,
        compiler_params=pltpu.CompilerParams(vmem_limit_bytes=16 * 2**20),
        cost_estimate=pl.CostEstimate(flops=10**7, bytes_accessed=8 * 2**20, transcendentals=0),
    )(branches, short_taps, skip)
    send, first_query, first_direct = pl.pallas_call(
        pack_kernel,
        grid=(1,),
        out_shape=[
            jax.ShapeDtypeStruct((PARTS, 2 * HALF, LANES), bf16),
            jax.ShapeDtypeStruct((CHANNELS, LANES), f32),
            jax.ShapeDtypeStruct((CHANNELS, LANES), f32),
        ],
        in_specs=[
            whole(3, CHANNELS, LANES),
            whole(3, CHANNELS, LANES),
            whole(3, CHANNELS, TAPS),
            whole(CHANNELS, 1),
            whole(CHANNELS * BLOCKS, LANES),
        ]
        + [whole(FILTERS, TOKENS)] * 4,
        out_specs=[whole(PARTS, 2 * HALF, LANES), whole(CHANNELS, LANES), whole(CHANNELS, LANES)],
        scratch_shapes=[pltpu.VMEM((CHANNELS * BLOCKS, LANES), f32)],
        compiler_params=pltpu.CompilerParams(vmem_limit_bytes=16 * 2**20),
    )(branches, tails, short_taps, skip, rows, *filters)
    data = lax.all_to_all(send, "ctx", 0, 0, tiled=True)
    conv = pl.pallas_call(
        conv_kernel,
        out_shape=jax.ShapeDtypeStruct((PARTS, HALF, LANES), bf16),
        in_specs=[VMEM],
        out_specs=VMEM,
        scratch_shapes=[
            pltpu.VMEM((2 * GROUP + ROWS, LANES), f32),
            pltpu.VMEM((OWN, ROWS, LANES), f32),
            pltpu.VMEM((OWN, 2, ROWS, GROUP * WIDTH), bf16),
            pltpu.VMEM((GROUP * WIDTH, 2 * LANES), bf16),
            pltpu.VMEM((GROUP * WIDTH, 2 * LANES), bf16),
            pltpu.VMEM((OWN, 2, 2 * GROUP + ROWS, 2 * LANES), f32),
        ],
        compiler_params=pltpu.CompilerParams(vmem_limit_bytes=32 * 2**20),
    )(data)
    conv = lax.all_to_all(conv, "ctx", 0, 0, tiled=True)
    return pl.pallas_call(
        mix_kernel,
        out_shape=jax.ShapeDtypeStruct((CHANNELS, TOKENS), bf16),
        in_specs=[VMEM] * 5,
        out_specs=VMEM,
        scratch_shapes=[pltpu.VMEM((CHANNELS * BLOCKS, LANES), f32)],
        compiler_params=pltpu.CompilerParams(vmem_limit_bytes=32 * 2**20),
    )(conv, query, direct, first_query, first_direct)


def solution(mesh):
    placed = (P(None, "ch", "ctx"), P(None, "ch", None), P("ch", "ctx"), P("ch"))
    return jax.shard_map(
        on_device, mesh=mesh, in_specs=placed, out_specs=P("ch", "ctx"), check_vma=False
    )
```

```python
import jax
import jax.numpy as jnp
from jax import lax
from jax.experimental import pallas as pl
from jax.experimental.pallas import tpu as pltpu
from jax.sharding import PartitionSpec as P

f32, bf16 = jnp.float32, jnp.bfloat16
LANES = 128
TAPS = 7
REACH = TAPS - 1
CHANNELS = 64
TOKENS = 2048
BLOCKS = TOKENS // LANES
PARTS = 32
FILTERS = 16
OWN = CHANNELS // PARTS
ROWS = PARTS * BLOCKS
HALF = OWN * BLOCKS
EDGE = 8
LOW, SKIP = 48, 96
STEP = 16
GROUP = 8
WIDTH = LANES // 2
VMEM = pl.BlockSpec(memory_space=pltpu.VMEM)


def prepare_kernel(
    all_filters_ref, all_taps_ref, all_skip_ref, all_branches_ref, cast_ref, taps_ref, skip_ref, branches_ref,
    filters_ref, rows_ref, semaphores,
):
    sources = (all_filters_ref, all_taps_ref, all_skip_ref, all_branches_ref)
    targets = (filters_ref, taps_ref, skip_ref, branches_ref)
    copies = [
        pltpu.make_async_copy(source, target, semaphores.at[at])
        for at, (source, target) in enumerate(zip(sources, targets))
    ]
    for copy in copies:
        copy.start()
    copies[0].wait()
    for block in range(BLOCKS):
        rows_ref[pl.ds(block, FILTERS, stride=BLOCKS), :] = filters_ref[:, block * LANES : (block + 1) * LANES]
    cast_ref[...] = rows_ref[...].reshape(FILTERS, BLOCKS, LANES).astype(bf16)
    for copy in copies[1:]:
        copy.wait()


def short_kernel(
    branch_ref, taps_ref, skip_ref, signal_ref, edge_ref, query_ref, direct_ref, rows_ref, edges_ref, small_ref, columns_ref
):
    small_ref[...] = jnp.zeros(small_ref.shape, f32)
    for branch in range(3):
        small_ref[8 * branch : 8 * branch + TAPS, :CHANNELS] = taps_ref[branch]
    small_ref[24:25, :CHANNELS] = skip_ref[...]
    columns_ref[...] = small_ref[...].T
    lane = lax.broadcasted_iota(jnp.int32, (STEP, LANES), 1)
    first = lane < REACH

    def body(index, carry):
        rows = pl.ds(pl.multiple_of(index * STEP, STEP), STEP)
        columns = columns_ref[rows, :]

        def column(at):
            return jnp.broadcast_to(columns[:, at : at + 1], (STEP, LANES))

        def filtered(branch):
            taps = [column(8 * branch + tap) for tap in range(TAPS)]
            before = [jnp.zeros((STEP, LANES), f32)] * REACH
            for block in range(BLOCKS):
                own = branch_ref[branch, rows, block * LANES : (block + 1) * LANES].astype(f32)
                total = taps[0] * own
                for tap in range(1, TAPS):
                    turned = pltpu.roll(own, tap, 1)
                    total += taps[tap] * jnp.where(lane < tap, before[tap - 1], turned)
                    before[tap - 1] = turned
                if block == 0:
                    edges_ref[branch, rows, :] = total
                yield total

        skip = column(24)
        for branch in (1, 2, 0):
            for block, total in enumerate(filtered(branch)):
                at = slice(block * LANES, (block + 1) * LANES)
                if branch == 1:
                    direct_ref[rows, at] = total
                elif branch == 2:
                    gated = direct_ref[rows, at] * total
                    direct_ref[rows, at] = skip * gated
                    rows_ref[pl.ds(index * (STEP * BLOCKS) + block, STEP, stride=BLOCKS), :] = gated
                else:
                    direct = total * direct_ref[rows, at]
                    query_ref[rows, at] = total if block else jnp.where(first, 1.0, total)
                    direct_ref[rows, at] = direct if block else jnp.where(first, 0.0, direct)
        return carry

    lax.fori_loop(0, CHANNELS // STEP, body, 0)
    signal_ref[...] = rows_ref[...].reshape(PARTS, HALF, LANES).astype(bf16)
    lane = lax.broadcasted_iota(jnp.int32, (CHANNELS, LANES), 1)
    edge = jnp.zeros((CHANNELS, LANES), f32)
    for branch in range(3):
        edge += pltpu.roll(jnp.where(lane < REACH, edges_ref[branch], 0.0), 8 * branch, 1)
        place = 24 + 8 * branch
        last = branch_ref[branch, :, TOKENS - LANES :].astype(f32)
        for tap in range(1, TAPS):
            weight = columns_ref[:CHANNELS, 8 * branch + tap : 8 * branch + tap + 1]
            share = weight * pltpu.roll(last, place + tap, 1)
            edge += jnp.where((lane >= place) & (lane < place + tap), share, 0.0)
    skip = columns_ref[:CHANNELS, 24:25]
    high = edge.astype(bf16).astype(f32)
    skip_high = skip.astype(bf16).astype(f32)
    gains = jnp.where(lane < SKIP, 0.0, jnp.where(lane < SKIP + 8, skip_high, skip - skip_high))
    edges_ref[0] = high + pltpu.roll(edge - high, LOW, 1) + gains
    rows_ref[: PARTS * EDGE, :] = jnp.zeros((PARTS * EDGE, LANES), f32)
    for own in range(OWN):
        rows_ref[pl.ds(own, PARTS, stride=EDGE), :] = edges_ref[0, pl.ds(own, PARTS, stride=OWN), :]
    edge_ref[...] = rows_ref[: PARTS * EDGE, :].reshape(PARTS, EDGE, LANES).astype(bf16)


def pack_kernel(signal_ref, edge_ref, own_ref, one_ref, two_ref, three_ref, send_ref):
    send_ref[:, :HALF, :] = signal_ref[...]
    send_ref[:, 2 * HALF :, :] = edge_ref[...]
    here = lax.axis_index("ch")
    owned = FILTERS // OWN
    for apart, taps_from in enumerate((own_ref, one_ref, two_ref, three_ref)):
        begin = pl.multiple_of((here ^ apart) * owned, owned)
        send_ref[pl.ds(begin, owned), HALF : 2 * HALF, :] = taps_from[...].reshape(owned, HALF, LANES)


def conv_kernel(data_ref, out_ref, signal_ref, taps_ref, edge_ref, left_ref, even_ref, odd_ref, sum_ref):
    shift = 2 * GROUP
    groups = ROWS // shift
    row = lax.broadcasted_iota(jnp.int32, (WIDTH, LANES), 0)
    lane = lax.broadcasted_iota(jnp.int32, (WIDTH, LANES), 1)
    above = lane >= row
    low = lax.broadcasted_iota(jnp.int32, (ROWS, LANES), 1) < WIDTH
    right = (even_ref, odd_ref)
    previous = jnp.zeros((WIDTH, LANES), f32)
    first = lax.broadcasted_iota(jnp.int32, (PARTS, LANES), 1) < REACH
    start = lax.broadcasted_iota(jnp.int32, (PARTS, LANES), 0) == 0
    edge_ref[...] = data_ref[:, 2 * HALF :, :].reshape(PARTS * EDGE, LANES).astype(f32)
    opening = pl.ds(shift, PARTS, stride=BLOCKS)

    def turn_back(value, by):
        return pltpu.roll(value, LANES - by, 1)

    def edges(own):
        row = edge_ref[pl.ds(own, PARTS, stride=EDGE), :]
        share = row + turn_back(row, LOW)
        other = jnp.where(start, 0.0, pltpu.roll(turn_back(share, 24), 1, 0))
        short = share + other
        gain = turn_back(row, SKIP) + turn_back(row, SKIP + 8)
        return short, turn_back(short, 8) * turn_back(short, 16), gain

    def load(own):
        begin = own * BLOCKS
        signal_ref[:shift, :] = jnp.zeros((shift, LANES), f32)
        signal_ref[shift:, :] = data_ref[:, begin : begin + BLOCKS, :].reshape(ROWS, LANES).astype(f32)
        signal_ref[opening, :] = jnp.where(first, edges(own)[1], signal_ref[opening, :])
        taps = data_ref[:, HALF + begin : HALF + begin + BLOCKS, :]
        taps_ref[own] = taps.reshape(ROWS, LANES).astype(f32)
        for lag in range(0, GROUP, 2):
            near = signal_ref[shift - 2 * lag : shift - 2 * lag + ROWS, :]
            far = signal_ref[shift - 2 * lag - 2 : shift - 2 * lag - 2 + ROWS, :]
            columns = slice(lag * WIDTH, (lag + 2) * WIDTH)
            left_ref[own, 0, :, columns] = jnp.where(low, near, pltpu.roll(far, WIDTH, 1)).astype(bf16)
            left_ref[own, 1, :, columns] = jnp.where(low, pltpu.roll(near, WIDTH, 1), far).astype(bf16)

    def toeplitz(step, lag, previous):
        own, group = divmod(step, groups)
        block = group * shift + lag
        if block == 0:
            previous = jnp.zeros((WIDTH, LANES), f32)
        current = jnp.broadcast_to(taps_ref[own, block : block + 1, :], (WIDTH, LANES))
        current = pltpu.roll(current, 0, 1, stride=1, stride_axis=0)
        right[step % 2][
            (lag // 2) * WIDTH : (lag // 2 + 1) * WIDTH, (lag % 2) * LANES : (lag % 2 + 1) * LANES
        ] = jnp.where(above, current, previous).astype(bf16)
        return current

    def finish(own):
        sums = sum_ref.at[own]
        for half in range(2):
            sums[half, :shift, :] = jnp.zeros((shift, 2 * LANES), f32)

        def gather(half, back):
            here, there = shift - back, shift - back - 1
            return sums[half, here : here + ROWS, :LANES] + sums[half, there : there + ROWS, LANES:]

        turned = jnp.where(low, pltpu.roll(gather(1, 1), WIDTH, 1), pltpu.roll(gather(1, 0), WIDTH, 1))
        signal_ref[shift:, :] = gather(0, 0) + turned
        query, gated, gain = edges(own)
        conv = signal_ref[opening, :]
        signal_ref[opening, :] = jnp.where(first, query * (conv + gain * gated), conv)
        result = signal_ref[shift:, :].astype(bf16).reshape(PARTS, BLOCKS, LANES)
        out_ref[:, own * BLOCKS : (own + 1) * BLOCKS, :] = result

    for own in range(OWN):
        load(own)
    for lag in range(shift):
        previous = toeplitz(0, lag, previous)
    steps = OWN * groups
    for step in range(steps):
        own, group = divmod(step, groups)
        for half in range(2):
            if step + 1 < steps:
                for lag in range(half * GROUP, (half + 1) * GROUP):
                    previous = toeplitz(step + 1, lag, previous)
            product = jnp.dot(
                left_ref[own, half, : ROWS - shift * group, :], right[step % 2][...], preferred_element_type=f32
            )
            if group == 0:
                sum_ref[own, half, shift:, :] = product
            else:
                sum_ref[own, half, shift + shift * group :, :] += product
        if group == groups - 1:
            finish(own)


def mix_kernel(conv_ref, query_ref, direct_ref, out_ref, rows_ref):
    rows_ref[...] = conv_ref[...].reshape(CHANNELS * BLOCKS, LANES).astype(f32)
    for block in range(BLOCKS):
        at = slice(block * LANES, (block + 1) * LANES)
        conv = rows_ref[pl.ds(block, CHANNELS, stride=BLOCKS), :]
        out_ref[:, at] = (query_ref[:, at] * conv + direct_ref[:, at]).astype(bf16)


def in_hbm(array):
    return pltpu.with_memory_space_constraint(array, pltpu.HBM)


def on_device(branches, short_taps, long_filter, skip_gain):
    own_filters, taps, skip, branches = pl.pallas_call(
        prepare_kernel,
        out_shape=[
            jax.ShapeDtypeStruct((FILTERS, BLOCKS, LANES), bf16),
            jax.ShapeDtypeStruct((3, TAPS, CHANNELS), f32),
            jax.ShapeDtypeStruct((1, CHANNELS), f32),
            jax.ShapeDtypeStruct((3, CHANNELS, TOKENS), bf16),
        ],
        in_specs=[pl.BlockSpec(memory_space=pltpu.HBM)] * 4,
        out_specs=[VMEM] * 4,
        scratch_shapes=[
            pltpu.VMEM((FILTERS, TOKENS), f32),
            pltpu.VMEM((FILTERS * BLOCKS, LANES), f32),
            pltpu.SemaphoreType.DMA((4,)),
        ],
        compiler_params=pltpu.CompilerParams(vmem_limit_bytes=8 * 2**20),
    )(in_hbm(long_filter), in_hbm(short_taps.transpose(0, 2, 1)), in_hbm(skip_gain[None, :]), in_hbm(branches))
    filters = [own_filters] + [
        lax.ppermute(own_filters, "ch", [(i, i ^ apart) for i in range(4)]) for apart in (1, 2, 3)
    ]
    signal, edge, query, direct = pl.pallas_call(
        short_kernel,
        out_shape=[
            jax.ShapeDtypeStruct((PARTS, HALF, LANES), bf16),
            jax.ShapeDtypeStruct((PARTS, EDGE, LANES), bf16),
            jax.ShapeDtypeStruct((CHANNELS, TOKENS), f32),
            jax.ShapeDtypeStruct((CHANNELS, TOKENS), f32),
        ],
        in_specs=[VMEM] * 3,
        out_specs=[VMEM] * 4,
        scratch_shapes=[
            pltpu.VMEM((CHANNELS * BLOCKS, LANES), f32),
            pltpu.VMEM((3, CHANNELS, LANES), f32),
            pltpu.VMEM((LANES, LANES), f32),
            pltpu.VMEM((LANES, LANES), f32),
        ],
        compiler_params=pltpu.CompilerParams(vmem_limit_bytes=16 * 2**20),
        cost_estimate=pl.CostEstimate(flops=10**7, bytes_accessed=8 * 2**20, transcendentals=0),
    )(branches, taps, skip)
    send = pl.pallas_call(
        pack_kernel,
        out_shape=jax.ShapeDtypeStruct((PARTS, 2 * HALF + EDGE, LANES), bf16),
        in_specs=[VMEM] * 6,
        out_specs=VMEM,
        compiler_params=pltpu.CompilerParams(vmem_limit_bytes=16 * 2**20),
    )(signal, edge, *filters)
    data = lax.all_to_all(send, "ctx", 0, 0, tiled=True)
    conv = pl.pallas_call(
        conv_kernel,
        out_shape=jax.ShapeDtypeStruct((PARTS, HALF, LANES), bf16),
        in_specs=[VMEM],
        out_specs=VMEM,
        scratch_shapes=[
            pltpu.VMEM((2 * GROUP + ROWS, LANES), f32),
            pltpu.VMEM((OWN, ROWS, LANES), f32),
            pltpu.VMEM((PARTS * EDGE, LANES), f32),
            pltpu.VMEM((OWN, 2, ROWS, GROUP * WIDTH), bf16),
            pltpu.VMEM((GROUP * WIDTH, 2 * LANES), bf16),
            pltpu.VMEM((GROUP * WIDTH, 2 * LANES), bf16),
            pltpu.VMEM((OWN, 2, 2 * GROUP + ROWS, 2 * LANES), f32),
        ],
        compiler_params=pltpu.CompilerParams(vmem_limit_bytes=32 * 2**20),
    )(data)
    conv = lax.all_to_all(conv, "ctx", 0, 0, tiled=True)
    return pl.pallas_call(
        mix_kernel,
        out_shape=jax.ShapeDtypeStruct((CHANNELS, TOKENS), bf16),
        in_specs=[VMEM] * 3,
        out_specs=VMEM,
        scratch_shapes=[pltpu.VMEM((CHANNELS * BLOCKS, LANES), f32)],
        compiler_params=pltpu.CompilerParams(vmem_limit_bytes=32 * 2**20),
    )(conv, query, direct)


def solution(mesh):
    placed = (P(None, "ch", "ctx"), P(None, "ch", None), P("ch", "ctx"), P("ch"))
    return jax.shard_map(
        on_device, mesh=mesh, in_specs=placed, out_specs=P("ch", "ctx"), check_vma=False
    )
```

```python
import jax
import jax.numpy as jnp
from jax import lax
from jax.experimental import pallas as pl
from jax.experimental.pallas import tpu as pltpu
from jax.sharding import PartitionSpec as P

f32, bf16 = jnp.float32, jnp.bfloat16
LANES = 128
TAPS = 7
REACH = TAPS - 1
CHANNELS = 64
TOKENS = 2048
BLOCKS = TOKENS // LANES
PARTS = 32
FILTERS = 16
OWN = CHANNELS // PARTS
ROWS = PARTS * BLOCKS
HALF = OWN * BLOCKS
EDGE = 8
LOW, SKIP = 48, 96
STEP = 16
GROUP = 8
WIDTH = LANES // 2
VMEM = pl.BlockSpec(memory_space=pltpu.VMEM)


def prepare_kernel(
    all_filters_ref, all_taps_ref, all_skip_ref, cast_ref, taps_ref, skip_ref, filters_ref, rows_ref, semaphores
):
    sources = (all_filters_ref, all_taps_ref, all_skip_ref)
    targets = (filters_ref, taps_ref, skip_ref)
    copies = [
        pltpu.make_async_copy(source, target, semaphores.at[at])
        for at, (source, target) in enumerate(zip(sources, targets))
    ]
    for copy in copies:
        copy.start()
    copies[0].wait()
    for block in range(BLOCKS):
        rows_ref[pl.ds(block, FILTERS, stride=BLOCKS), :] = filters_ref[:, block * LANES : (block + 1) * LANES]
    cast_ref[...] = rows_ref[...].reshape(FILTERS, BLOCKS, LANES).astype(bf16)
    for copy in copies[1:]:
        copy.wait()


def short_kernel(
    branches_ref, taps_ref, skip_ref, signal_ref, edge_ref, query_ref, direct_ref,
    branch_ref, semaphores, rows_ref, edges_ref, small_ref, columns_ref,
):
    def fetch(index):
        rows = pl.ds(pl.multiple_of(index * STEP, STEP), STEP)
        return pltpu.make_async_copy(branches_ref.at[:, rows, :], branch_ref.at[:, rows, :], semaphores.at[index])

    for index in range(CHANNELS // STEP):
        fetch(index).start()
    small_ref[...] = jnp.zeros(small_ref.shape, f32)
    for branch in range(3):
        small_ref[8 * branch : 8 * branch + TAPS, :CHANNELS] = taps_ref[branch]
    small_ref[24:25, :CHANNELS] = skip_ref[...]
    columns_ref[...] = small_ref[...].T
    lane = lax.broadcasted_iota(jnp.int32, (STEP, LANES), 1)
    first = lane < REACH

    def body(index, carry):
        rows = pl.ds(pl.multiple_of(index * STEP, STEP), STEP)
        columns = columns_ref[rows, :]
        fetch(index).wait()

        def column(at):
            return jnp.broadcast_to(columns[:, at : at + 1], (STEP, LANES))

        def filtered(branch):
            taps = [column(8 * branch + tap) for tap in range(TAPS)]
            before = [jnp.zeros((STEP, LANES), f32)] * REACH
            for block in range(BLOCKS):
                own = branch_ref[branch, rows, block * LANES : (block + 1) * LANES].astype(f32)
                total = taps[0] * own
                for tap in range(1, TAPS):
                    turned = pltpu.roll(own, tap, 1)
                    total += taps[tap] * jnp.where(lane < tap, before[tap - 1], turned)
                    before[tap - 1] = turned
                if block == 0:
                    edges_ref[branch, rows, :] = total
                yield total

        skip = column(24)
        for branch in (1, 2, 0):
            for block, total in enumerate(filtered(branch)):
                at = slice(block * LANES, (block + 1) * LANES)
                if branch == 1:
                    direct_ref[rows, at] = total
                elif branch == 2:
                    gated = direct_ref[rows, at] * total
                    direct_ref[rows, at] = skip * gated
                    rows_ref[pl.ds(index * (STEP * BLOCKS) + block, STEP, stride=BLOCKS), :] = gated
                else:
                    direct = total * direct_ref[rows, at]
                    query_ref[rows, at] = total if block else jnp.where(first, 1.0, total)
                    direct_ref[rows, at] = direct if block else jnp.where(first, 0.0, direct)
        return carry

    lax.fori_loop(0, CHANNELS // STEP, body, 0)
    signal_ref[...] = rows_ref[...].reshape(PARTS, HALF, LANES).astype(bf16)
    lane = lax.broadcasted_iota(jnp.int32, (CHANNELS, LANES), 1)
    edge = jnp.zeros((CHANNELS, LANES), f32)
    for branch in range(3):
        edge += pltpu.roll(jnp.where(lane < REACH, edges_ref[branch], 0.0), 8 * branch, 1)
        place = 24 + 8 * branch
        last = branch_ref[branch, :, TOKENS - LANES :].astype(f32)
        for tap in range(1, TAPS):
            weight = columns_ref[:CHANNELS, 8 * branch + tap : 8 * branch + tap + 1]
            share = weight * pltpu.roll(last, place + tap, 1)
            edge += jnp.where((lane >= place) & (lane < place + tap), share, 0.0)
    skip = columns_ref[:CHANNELS, 24:25]
    high = edge.astype(bf16).astype(f32)
    skip_high = skip.astype(bf16).astype(f32)
    gains = jnp.where(lane < SKIP, 0.0, jnp.where(lane < SKIP + 8, skip_high, skip - skip_high))
    edges_ref[0] = high + pltpu.roll(edge - high, LOW, 1) + gains
    rows_ref[: PARTS * EDGE, :] = jnp.zeros((PARTS * EDGE, LANES), f32)
    for own in range(OWN):
        rows_ref[pl.ds(own, PARTS, stride=EDGE), :] = edges_ref[0, pl.ds(own, PARTS, stride=OWN), :]
    edge_ref[...] = rows_ref[: PARTS * EDGE, :].reshape(PARTS, EDGE, LANES).astype(bf16)


def pack_kernel(signal_ref, edge_ref, own_ref, one_ref, two_ref, three_ref, send_ref):
    send_ref[:, :HALF, :] = signal_ref[...]
    send_ref[:, 2 * HALF :, :] = edge_ref[...]
    here = lax.axis_index("ch")
    owned = FILTERS // OWN
    for apart, taps_from in enumerate((own_ref, one_ref, two_ref, three_ref)):
        begin = pl.multiple_of((here ^ apart) * owned, owned)
        send_ref[pl.ds(begin, owned), HALF : 2 * HALF, :] = taps_from[...].reshape(owned, HALF, LANES)


def conv_kernel(data_ref, out_ref, signal_ref, taps_ref, edge_ref, left_ref, even_ref, odd_ref, sum_ref):
    shift = 2 * GROUP
    groups = ROWS // shift
    row = lax.broadcasted_iota(jnp.int32, (WIDTH, LANES), 0)
    lane = lax.broadcasted_iota(jnp.int32, (WIDTH, LANES), 1)
    above = lane >= row
    low = lax.broadcasted_iota(jnp.int32, (ROWS, LANES), 1) < WIDTH
    right = (even_ref, odd_ref)
    previous = jnp.zeros((WIDTH, LANES), f32)
    first = lax.broadcasted_iota(jnp.int32, (PARTS, LANES), 1) < REACH
    start = lax.broadcasted_iota(jnp.int32, (PARTS, LANES), 0) == 0
    edge_ref[...] = data_ref[:, 2 * HALF :, :].reshape(PARTS * EDGE, LANES).astype(f32)
    opening = pl.ds(shift, PARTS, stride=BLOCKS)

    def turn_back(value, by):
        return pltpu.roll(value, LANES - by, 1)

    def edges(own):
        row = edge_ref[pl.ds(own, PARTS, stride=EDGE), :]
        share = row + turn_back(row, LOW)
        other = jnp.where(start, 0.0, pltpu.roll(turn_back(share, 24), 1, 0))
        short = share + other
        gain = turn_back(row, SKIP) + turn_back(row, SKIP + 8)
        return short, turn_back(short, 8) * turn_back(short, 16), gain

    def load(own):
        begin = own * BLOCKS
        signal_ref[:shift, :] = jnp.zeros((shift, LANES), f32)
        signal_ref[shift:, :] = data_ref[:, begin : begin + BLOCKS, :].reshape(ROWS, LANES).astype(f32)
        signal_ref[opening, :] = jnp.where(first, edges(own)[1], signal_ref[opening, :])
        taps = data_ref[:, HALF + begin : HALF + begin + BLOCKS, :]
        taps_ref[own] = taps.reshape(ROWS, LANES).astype(f32)
        yield
        for lag in range(0, GROUP, 2):
            near = signal_ref[shift - 2 * lag : shift - 2 * lag + ROWS, :]
            far = signal_ref[shift - 2 * lag - 2 : shift - 2 * lag - 2 + ROWS, :]
            columns = slice(lag * WIDTH, (lag + 2) * WIDTH)
            left_ref[own, 0, :, columns] = jnp.where(low, near, pltpu.roll(far, WIDTH, 1)).astype(bf16)
            left_ref[own, 1, :, columns] = jnp.where(low, pltpu.roll(near, WIDTH, 1), far).astype(bf16)
            yield

    def toeplitz(step, lag, previous):
        own, group = divmod(step, groups)
        block = group * shift + lag
        if block == 0:
            previous = jnp.zeros((WIDTH, LANES), f32)
        current = jnp.broadcast_to(taps_ref[own, block : block + 1, :], (WIDTH, LANES))
        current = pltpu.roll(current, 0, 1, stride=1, stride_axis=0)
        right[step % 2][
            (lag // 2) * WIDTH : (lag // 2 + 1) * WIDTH, (lag % 2) * LANES : (lag % 2 + 1) * LANES
        ] = jnp.where(above, current, previous).astype(bf16)
        return current

    def finish(own):
        sums = sum_ref.at[own]
        for half in range(2):
            sums[half, :shift, :] = jnp.zeros((shift, 2 * LANES), f32)

        def gather(half, back):
            here, there = shift - back, shift - back - 1
            return sums[half, here : here + ROWS, :LANES] + sums[half, there : there + ROWS, LANES:]

        turned = jnp.where(low, pltpu.roll(gather(1, 1), WIDTH, 1), pltpu.roll(gather(1, 0), WIDTH, 1))
        signal_ref[shift:, :] = gather(0, 0) + turned
        query, gated, gain = edges(own)
        conv = signal_ref[opening, :]
        signal_ref[opening, :] = jnp.where(first, query * (conv + gain * gated), conv)
        result = signal_ref[shift:, :].astype(bf16).reshape(PARTS, BLOCKS, LANES)
        out_ref[:, own * BLOCKS : (own + 1) * BLOCKS, :] = result

    for _ in load(0):
        pass
    loads = [load(own) for own in range(1, OWN)]
    for lag in range(shift):
        previous = toeplitz(0, lag, previous)
    steps = OWN * groups
    for step in range(steps):
        own, group = divmod(step, groups)
        for half in range(2):
            if step + 1 < steps:
                for lag in range(half * GROUP, (half + 1) * GROUP):
                    previous = toeplitz(step + 1, lag, previous)
            if half and own + 1 < OWN:
                next(loads[own], None)
            product = jnp.dot(
                left_ref[own, half, : ROWS - shift * group, :], right[step % 2][...], preferred_element_type=f32
            )
            if group == 0:
                sum_ref[own, half, shift:, :] = product
            else:
                sum_ref[own, half, shift + shift * group :, :] += product
        if group == groups - 1:
            finish(own)


def mix_kernel(conv_ref, query_ref, direct_ref, out_ref, rows_ref):
    rows_ref[...] = conv_ref[...].reshape(CHANNELS * BLOCKS, LANES).astype(f32)
    for block in range(BLOCKS):
        at = slice(block * LANES, (block + 1) * LANES)
        conv = rows_ref[pl.ds(block, CHANNELS, stride=BLOCKS), :]
        out_ref[:, at] = (query_ref[:, at] * conv + direct_ref[:, at]).astype(bf16)


def in_hbm(array):
    return pltpu.with_memory_space_constraint(array, pltpu.HBM)


def on_device(branches, short_taps, long_filter, skip_gain):
    own_filters, taps, skip = pl.pallas_call(
        prepare_kernel,
        out_shape=[
            jax.ShapeDtypeStruct((FILTERS, BLOCKS, LANES), bf16),
            jax.ShapeDtypeStruct((3, TAPS, CHANNELS), f32),
            jax.ShapeDtypeStruct((1, CHANNELS), f32),
        ],
        in_specs=[pl.BlockSpec(memory_space=pltpu.HBM)] * 3,
        out_specs=[VMEM] * 3,
        scratch_shapes=[
            pltpu.VMEM((FILTERS, TOKENS), f32),
            pltpu.VMEM((FILTERS * BLOCKS, LANES), f32),
            pltpu.SemaphoreType.DMA((3,)),
        ],
        compiler_params=pltpu.CompilerParams(vmem_limit_bytes=8 * 2**20),
    )(in_hbm(long_filter), in_hbm(short_taps.transpose(0, 2, 1)), in_hbm(skip_gain[None, :]))
    filters = [own_filters] + [
        lax.ppermute(own_filters, "ch", [(i, i ^ apart) for i in range(4)]) for apart in (1, 2, 3)
    ]
    signal, edge, query, direct = pl.pallas_call(
        short_kernel,
        out_shape=[
            jax.ShapeDtypeStruct((PARTS, HALF, LANES), bf16),
            jax.ShapeDtypeStruct((PARTS, EDGE, LANES), bf16),
            jax.ShapeDtypeStruct((CHANNELS, TOKENS), f32),
            jax.ShapeDtypeStruct((CHANNELS, TOKENS), f32),
        ],
        in_specs=[pl.BlockSpec(memory_space=pltpu.HBM), VMEM, VMEM],
        out_specs=[VMEM] * 4,
        scratch_shapes=[
            pltpu.VMEM((3, CHANNELS, TOKENS), bf16),
            pltpu.SemaphoreType.DMA((CHANNELS // STEP,)),
            pltpu.VMEM((CHANNELS * BLOCKS, LANES), f32),
            pltpu.VMEM((3, CHANNELS, LANES), f32),
            pltpu.VMEM((LANES, LANES), f32),
            pltpu.VMEM((LANES, LANES), f32),
        ],
        compiler_params=pltpu.CompilerParams(vmem_limit_bytes=16 * 2**20),
        cost_estimate=pl.CostEstimate(flops=10**7, bytes_accessed=8 * 2**20, transcendentals=0),
    )(in_hbm(branches), taps, skip)
    send = pl.pallas_call(
        pack_kernel,
        out_shape=jax.ShapeDtypeStruct((PARTS, 2 * HALF + EDGE, LANES), bf16),
        in_specs=[VMEM] * 6,
        out_specs=VMEM,
        compiler_params=pltpu.CompilerParams(vmem_limit_bytes=16 * 2**20),
    )(signal, edge, *filters)
    data = lax.all_to_all(send, "ctx", 0, 0, tiled=True)
    conv = pl.pallas_call(
        conv_kernel,
        out_shape=jax.ShapeDtypeStruct((PARTS, HALF, LANES), bf16),
        in_specs=[VMEM],
        out_specs=VMEM,
        scratch_shapes=[
            pltpu.VMEM((2 * GROUP + ROWS, LANES), f32),
            pltpu.VMEM((OWN, ROWS, LANES), f32),
            pltpu.VMEM((PARTS * EDGE, LANES), f32),
            pltpu.VMEM((OWN, 2, ROWS, GROUP * WIDTH), bf16),
            pltpu.VMEM((GROUP * WIDTH, 2 * LANES), bf16),
            pltpu.VMEM((GROUP * WIDTH, 2 * LANES), bf16),
            pltpu.VMEM((OWN, 2, 2 * GROUP + ROWS, 2 * LANES), f32),
        ],
        compiler_params=pltpu.CompilerParams(vmem_limit_bytes=32 * 2**20),
    )(data)
    conv = lax.all_to_all(conv, "ctx", 0, 0, tiled=True)
    return pl.pallas_call(
        mix_kernel,
        out_shape=jax.ShapeDtypeStruct((CHANNELS, TOKENS), bf16),
        in_specs=[VMEM] * 3,
        out_specs=VMEM,
        scratch_shapes=[pltpu.VMEM((CHANNELS * BLOCKS, LANES), f32)],
        compiler_params=pltpu.CompilerParams(vmem_limit_bytes=32 * 2**20),
    )(conv, query, direct)


def solution(mesh):
    placed = (P(None, "ch", "ctx"), P(None, "ch", None), P("ch", "ctx"), P("ch"))
    return jax.shard_map(
        on_device, mesh=mesh, in_specs=placed, out_specs=P("ch", "ctx"), check_vma=False
    )
```

```python
import jax
import jax.numpy as jnp
from jax import lax
from jax.experimental import pallas as pl
from jax.experimental.pallas import tpu as pltpu
from jax.sharding import PartitionSpec as P

f32, bf16 = jnp.float32, jnp.bfloat16
LANES = 128
TAPS = 7
REACH = TAPS - 1
CHANNELS = 64
TOKENS = 2048
BLOCKS = TOKENS // LANES
PARTS = 32
FILTERS = 16
OWN = CHANNELS // PARTS
ROWS = PARTS * BLOCKS
HALF = OWN * BLOCKS
EDGES_AT = HALF + BLOCKS
EDGE = 8
LOW, SKIP = 48, 96
STEP = 16
GROUP = 8
WIDTH = LANES // 2
VMEM = pl.BlockSpec(memory_space=pltpu.VMEM)


def prepare_kernel(
    all_filters_ref, all_taps_ref, all_skip_ref, all_branches_ref, same_ref, other_ref, taps_ref, skip_ref, branches_ref,
    filters_ref, rows_ref, semaphores,
):
    sources = (all_filters_ref, all_taps_ref, all_skip_ref, all_branches_ref)
    targets = (filters_ref, taps_ref, skip_ref, branches_ref)
    copies = [
        pltpu.make_async_copy(source, target, semaphores.at[at])
        for at, (source, target) in enumerate(zip(sources, targets))
    ]
    for copy in copies:
        copy.start()
    copies[0].wait()
    for block in range(BLOCKS):
        rows_ref[pl.ds(block, FILTERS, stride=BLOCKS), :] = filters_ref[:, block * LANES : (block + 1) * LANES]
    rows = rows_ref[...].reshape(FILTERS // 2, 2, BLOCKS, LANES)
    second = lax.rem(lax.axis_index("ch"), 2) == 1
    same_ref[...] = jnp.where(second, rows[:, 1], rows[:, 0]).astype(bf16)
    other_ref[...] = jnp.where(second, rows[:, 0], rows[:, 1]).astype(bf16)
    for copy in copies[1:]:
        copy.wait()


def stand(columns_ref, small_ref, taps_ref, skip_ref):
    small_ref[...] = jnp.zeros(small_ref.shape, f32)
    for branch in range(3):
        small_ref[8 * branch : 8 * branch + TAPS, :CHANNELS] = taps_ref[branch]
    small_ref[24:25, :CHANNELS] = skip_ref[...]
    columns_ref[...] = small_ref[...].T


def filtered(branch_ref, columns, branch, rows):
    lane = lax.broadcasted_iota(jnp.int32, (STEP, LANES), 1)
    taps = [jnp.broadcast_to(columns[:, 8 * branch + tap : 8 * branch + tap + 1], (STEP, LANES)) for tap in range(TAPS)]
    before = [jnp.zeros((STEP, LANES), f32)] * REACH
    for block in range(BLOCKS):
        own = branch_ref[branch, rows, block * LANES : (block + 1) * LANES].astype(f32)
        total = taps[0] * own
        for tap in range(1, TAPS):
            turned = pltpu.roll(own, tap, 1)
            total += taps[tap] * jnp.where(lane < tap, before[tap - 1], turned)
            before[tap - 1] = turned
        yield total


def short_kernel(
    branch_ref, taps_ref, skip_ref, signal_ref, edge_ref, query_ref, direct_ref, rows_ref, edges_ref, small_ref, columns_ref
):
    stand(columns_ref, small_ref, taps_ref, skip_ref)
    first = lax.broadcasted_iota(jnp.int32, (STEP, LANES), 1) < REACH

    def body(index, carry):
        rows = pl.ds(pl.multiple_of(index * STEP, STEP), STEP)
        columns = columns_ref[rows, :]
        skip = jnp.broadcast_to(columns[:, 24:25], (STEP, LANES))
        for block, total in enumerate(filtered(branch_ref, columns, 1, rows)):
            direct_ref[rows, block * LANES : (block + 1) * LANES] = total
            if block == 0:
                edges_ref[1, rows, :] = total
        for block, total in enumerate(filtered(branch_ref, columns, 2, rows)):
            at = slice(block * LANES, (block + 1) * LANES)
            gated = direct_ref[rows, at] * total
            direct_ref[rows, at] = skip * gated
            rows_ref[pl.ds(index * (STEP * BLOCKS) + block, STEP, stride=BLOCKS), :] = gated
            if block == 0:
                edges_ref[2, rows, :] = total
        for block, total in enumerate(filtered(branch_ref, columns, 0, rows)):
            at = slice(block * LANES, (block + 1) * LANES)
            direct = total * direct_ref[rows, at]
            query_ref[rows, at] = total if block else jnp.where(first, 1.0, total)
            direct_ref[rows, at] = direct if block else jnp.where(first, 0.0, direct)
            if block == 0:
                edges_ref[0, rows, :] = total
        return carry

    lax.fori_loop(0, CHANNELS // STEP, body, 0)
    signal_ref[...] = rows_ref[...].reshape(PARTS, HALF, LANES).astype(bf16)
    lane = lax.broadcasted_iota(jnp.int32, (CHANNELS, LANES), 1)
    edge = jnp.where(lane < REACH, edges_ref[0], 0.0)
    for branch in range(3):
        if branch:
            edge += pltpu.roll(jnp.where(lane < REACH, edges_ref[branch], 0.0), 8 * branch, 1)
        place = 24 + 8 * branch
        last = branch_ref[branch, :, TOKENS - LANES :].astype(f32)
        for tap in range(1, TAPS):
            weight = columns_ref[:CHANNELS, 8 * branch + tap : 8 * branch + tap + 1]
            share = weight * pltpu.roll(last, place + tap, 1)
            edge += jnp.where((lane >= place) & (lane < place + tap), share, 0.0)
    skip = columns_ref[:CHANNELS, 24:25]
    high = edge.astype(bf16).astype(f32)
    skip_high = skip.astype(bf16).astype(f32)
    gains = jnp.where(lane < SKIP, 0.0, jnp.where(lane < SKIP + 8, skip_high, skip - skip_high))
    edges_ref[0] = high + pltpu.roll(edge - high, LOW, 1) + gains
    rows_ref[: PARTS * EDGE, :] = jnp.zeros((PARTS * EDGE, LANES), f32)
    for own in range(OWN):
        rows_ref[pl.ds(own, PARTS, stride=EDGE), :] = edges_ref[0, pl.ds(own, PARTS, stride=OWN), :]
    edge_ref[...] = rows_ref[: PARTS * EDGE, :].reshape(PARTS, EDGE, LANES).astype(bf16)


def pack_kernel(signal_ref, edge_ref, own_ref, one_ref, two_ref, three_ref, send_ref):
    send_ref[:, :HALF, :] = signal_ref[...]
    send_ref[:, EDGES_AT:, :] = edge_ref[...]
    here = lax.axis_index("ch")
    owned = FILTERS // OWN
    for apart, taps_from in enumerate((own_ref, one_ref, two_ref, three_ref)):
        begin = pl.multiple_of((here ^ apart) * owned, owned)
        send_ref[pl.ds(begin, owned), HALF:EDGES_AT, :] = taps_from[...]


def conv_kernel(data_ref, *rest):
    *inputs, out_ref, signal_ref, taps_ref, edge_ref, left_ref, even_ref, odd_ref, sum_ref = rest
    core = lax.rem(lax.axis_index("ch"), 2)
    channel = 1 - core if inputs else core
    shift = 2 * GROUP
    groups = ROWS // shift
    row = lax.broadcasted_iota(jnp.int32, (WIDTH, LANES), 0)
    lane = lax.broadcasted_iota(jnp.int32, (WIDTH, LANES), 1)
    above = lane >= row
    low = lax.broadcasted_iota(jnp.int32, (ROWS, LANES), 1) < WIDTH
    right = (even_ref, odd_ref)
    previous = jnp.zeros((WIDTH, LANES), bf16)
    first = lax.broadcasted_iota(jnp.int32, (PARTS, LANES), 1) < REACH
    start = lax.broadcasted_iota(jnp.int32, (PARTS, LANES), 0) == 0
    edge_ref[...] = data_ref[:, EDGES_AT:, :].reshape(PARTS * EDGE, LANES).astype(f32)
    opening = pl.ds(shift, PARTS, stride=BLOCKS)

    def turn_back(value, by):
        return pltpu.roll(value, LANES - by, 1)

    def place(at):
        return pl.ds(pl.multiple_of(at * BLOCKS, BLOCKS), BLOCKS)

    def edges():
        rows = [edge_ref[pl.ds(at, PARTS, stride=EDGE), :] for at in range(OWN)]
        row = jnp.where(channel == 1, rows[1], rows[0])
        share = row + turn_back(row, LOW)
        other = jnp.where(start, 0.0, pltpu.roll(turn_back(share, 24), 1, 0))
        short = share + other
        gain = turn_back(row, SKIP) + turn_back(row, SKIP + 8)
        return short, turn_back(short, 8) * turn_back(short, 16), gain

    signal_ref[:shift, :] = jnp.zeros((shift, LANES), f32)
    signal_ref[shift:, :] = data_ref[:, place(channel), :].reshape(ROWS, LANES).astype(f32)
    signal_ref[opening, :] = jnp.where(first, edges()[1], signal_ref[opening, :])
    taps = inputs[0][...] if inputs else data_ref[:, HALF:EDGES_AT, :]
    taps_ref[...] = taps.reshape(ROWS, LANES).astype(f32)
    for lag in range(0, GROUP, 2):
        near = signal_ref[shift - 2 * lag : shift - 2 * lag + ROWS, :]
        far = signal_ref[shift - 2 * lag - 2 : shift - 2 * lag - 2 + ROWS, :]
        columns = slice(lag * WIDTH, (lag + 2) * WIDTH)
        left_ref[0, :, columns] = jnp.where(low, near, pltpu.roll(far, WIDTH, 1)).astype(bf16)
        left_ref[1, :, columns] = jnp.where(low, pltpu.roll(near, WIDTH, 1), far).astype(bf16)

    def toeplitz(group, lag, previous):
        block = group * shift + lag
        current = jnp.broadcast_to(taps_ref[block : block + 1, :], (WIDTH, LANES))
        current = pltpu.roll(current, 0, 1, stride=1, stride_axis=0).astype(bf16)
        right[group % 2][
            (lag // 2) * WIDTH : (lag // 2 + 1) * WIDTH, (lag % 2) * LANES : (lag % 2 + 1) * LANES
        ] = jnp.where(above, current, previous)
        return current

    for lag in range(shift):
        previous = toeplitz(0, lag, previous)
    for group in range(groups):
        for half in range(2):
            if group + 1 < groups:
                for lag in range(half * GROUP, (half + 1) * GROUP):
                    previous = toeplitz(group + 1, lag, previous)
            product = jnp.dot(
                left_ref[half, : ROWS - shift * group, :], right[group % 2][...], preferred_element_type=f32
            )
            if group == 0:
                sum_ref[half, shift:, :] = product
            else:
                sum_ref[half, shift + shift * group :, :] += product

    for half in range(2):
        sum_ref[half, :shift, :] = jnp.zeros((shift, 2 * LANES), f32)

    def gather(half, back):
        here, there = shift - back, shift - back - 1
        return sum_ref[half, here : here + ROWS, :LANES] + sum_ref[half, there : there + ROWS, LANES:]

    turned = jnp.where(low, pltpu.roll(gather(1, 1), WIDTH, 1), pltpu.roll(gather(1, 0), WIDTH, 1))
    signal_ref[shift:, :] = gather(0, 0) + turned
    query, gated, gain = edges()
    conv = signal_ref[opening, :]
    signal_ref[opening, :] = jnp.where(first, query * (conv + gain * gated), conv)
    result = signal_ref[shift:, :].astype(bf16).reshape(PARTS, BLOCKS, LANES)
    if inputs:
        out_ref[:, place(channel), :] = result
        out_ref[:, place(1 - channel), :] = inputs[1][...]
    else:
        out_ref[...] = result


def convolve(data, *inputs):
    return pl.pallas_call(
        conv_kernel,
        out_shape=jax.ShapeDtypeStruct((PARTS, HALF if inputs else BLOCKS, LANES), bf16),
        in_specs=[VMEM] * (1 + len(inputs)),
        out_specs=VMEM,
        scratch_shapes=[
            pltpu.VMEM((2 * GROUP + ROWS, LANES), f32),
            pltpu.VMEM((ROWS, LANES), f32),
            pltpu.VMEM((PARTS * EDGE, LANES), f32),
            pltpu.VMEM((2, ROWS, GROUP * WIDTH), bf16),
            pltpu.VMEM((GROUP * WIDTH, 2 * LANES), bf16),
            pltpu.VMEM((GROUP * WIDTH, 2 * LANES), bf16),
            pltpu.VMEM((2, 2 * GROUP + ROWS, 2 * LANES), f32),
        ],
        compiler_params=pltpu.CompilerParams(vmem_limit_bytes=16 * 2**20),
        cost_estimate=pl.CostEstimate(flops=4 * 10**9, bytes_accessed=2**20, transcendentals=0),
    )(data, *inputs)


def mix_kernel(conv_ref, query_ref, direct_ref, out_ref, rows_ref):
    rows_ref[...] = conv_ref[...].reshape(CHANNELS * BLOCKS, LANES).astype(f32)
    for block in range(BLOCKS):
        at = slice(block * LANES, (block + 1) * LANES)
        conv = rows_ref[pl.ds(block, CHANNELS, stride=BLOCKS), :]
        out_ref[:, at] = (query_ref[:, at] * conv + direct_ref[:, at]).astype(bf16)


def in_hbm(array):
    return pltpu.with_memory_space_constraint(array, pltpu.HBM)


def on_device(branches, short_taps, long_filter, skip_gain):
    same, other, taps, skip, branches = pl.pallas_call(
        prepare_kernel,
        out_shape=[
            jax.ShapeDtypeStruct((FILTERS // 2, BLOCKS, LANES), bf16),
            jax.ShapeDtypeStruct((FILTERS // 2, BLOCKS, LANES), bf16),
            jax.ShapeDtypeStruct((3, TAPS, CHANNELS), f32),
            jax.ShapeDtypeStruct((1, CHANNELS), f32),
            jax.ShapeDtypeStruct((3, CHANNELS, TOKENS), bf16),
        ],
        in_specs=[pl.BlockSpec(memory_space=pltpu.HBM)] * 4,
        out_specs=[VMEM] * 5,
        scratch_shapes=[
            pltpu.VMEM((FILTERS, TOKENS), f32),
            pltpu.VMEM((FILTERS * BLOCKS, LANES), f32),
            pltpu.SemaphoreType.DMA((4,)),
        ],
        compiler_params=pltpu.CompilerParams(vmem_limit_bytes=8 * 2**20),
    )(in_hbm(long_filter), in_hbm(short_taps.transpose(0, 2, 1)), in_hbm(skip_gain[None, :]), in_hbm(branches))
    filters = [same] + [
        lax.ppermute(sent, "ch", [(i, i ^ apart) for i in range(4)]) for apart, sent in ((1, other), (2, same), (3, other))
    ]
    signal, edge, query, direct = pl.pallas_call(
        short_kernel,
        out_shape=[
            jax.ShapeDtypeStruct((PARTS, HALF, LANES), bf16),
            jax.ShapeDtypeStruct((PARTS, EDGE, LANES), bf16),
            jax.ShapeDtypeStruct((CHANNELS, TOKENS), f32),
            jax.ShapeDtypeStruct((CHANNELS, TOKENS), f32),
        ],
        in_specs=[VMEM] * 3,
        out_specs=[VMEM] * 4,
        scratch_shapes=[
            pltpu.VMEM((CHANNELS * BLOCKS, LANES), f32),
            pltpu.VMEM((3, CHANNELS, LANES), f32),
            pltpu.VMEM((LANES, LANES), f32),
            pltpu.VMEM((LANES, LANES), f32),
        ],
        compiler_params=pltpu.CompilerParams(vmem_limit_bytes=16 * 2**20),
        cost_estimate=pl.CostEstimate(flops=10**7, bytes_accessed=8 * 2**20, transcendentals=0),
    )(branches, taps, skip)
    send = pl.pallas_call(
        pack_kernel,
        out_shape=jax.ShapeDtypeStruct((PARTS, EDGES_AT + EDGE, LANES), bf16),
        in_specs=[VMEM] * 6,
        out_specs=VMEM,
        compiler_params=pltpu.CompilerParams(vmem_limit_bytes=16 * 2**20),
    )(signal, edge, *filters)
    data = lax.all_to_all(send, "ctx", 0, 0, tiled=True)
    swapped = lax.ppermute(data[:, HALF:EDGES_AT, :], "ch", [(i, i ^ 1) for i in range(4)])
    conv = convolve(data, swapped, convolve(data))
    conv = lax.all_to_all(conv, "ctx", 0, 0, tiled=True)
    return pl.pallas_call(
        mix_kernel,
        out_shape=jax.ShapeDtypeStruct((CHANNELS, TOKENS), bf16),
        in_specs=[VMEM] * 3,
        out_specs=VMEM,
        scratch_shapes=[pltpu.VMEM((CHANNELS * BLOCKS, LANES), f32)],
        compiler_params=pltpu.CompilerParams(vmem_limit_bytes=32 * 2**20),
    )(conv, query, direct)


def solution(mesh):
    placed = (P(None, "ch", "ctx"), P(None, "ch", None), P("ch", "ctx"), P("ch"))
    return jax.shard_map(
        on_device, mesh=mesh, in_specs=placed, out_specs=P("ch", "ctx"), check_vma=False
    )
```

```python
import jax
import jax.numpy as jnp
from jax import lax
from jax.experimental import pallas as pl
from jax.experimental.pallas import tpu as pltpu
from jax.sharding import PartitionSpec as P

f32, bf16 = jnp.float32, jnp.bfloat16
LANES = 128
TAPS = 7
REACH = TAPS - 1
CHANNELS = 64
TOKENS = 2048
BLOCKS = TOKENS // LANES
PARTS = 32
FILTERS = 16
OWN = CHANNELS // PARTS
ROWS = PARTS * BLOCKS
HALF = OWN * BLOCKS
EDGES_AT = HALF + BLOCKS
EDGE = 8
LOW, SKIP = 48, 96
STEP = 16
GROUP = 8
WIDTH = LANES // 2
VMEM = pl.BlockSpec(memory_space=pltpu.VMEM)


def prepare_kernel(
    all_filters_ref, all_taps_ref, all_skip_ref, all_branches_ref, cast_ref, taps_ref, skip_ref, branches_ref,
    filters_ref, rows_ref, semaphores,
):
    sources = [all_filters_ref, all_taps_ref, all_skip_ref] + [all_branches_ref.at[branch] for branch in range(3)]
    targets = [filters_ref, taps_ref, skip_ref] + [branches_ref.at[branch] for branch in range(3)]
    copies = [
        pltpu.make_async_copy(source, target, semaphores.at[at])
        for at, (source, target) in enumerate(zip(sources, targets))
    ]
    for copy in copies:
        copy.start()
    copies[0].wait()
    for block in range(BLOCKS):
        rows_ref[pl.ds(block, FILTERS, stride=BLOCKS), :] = filters_ref[:, block * LANES : (block + 1) * LANES]
    cast_ref[...] = rows_ref[...].reshape(FILTERS, BLOCKS, LANES).astype(bf16)
    for copy in copies[1:]:
        copy.wait()


PLACES = [(chip, own) for chip in range(2) for own in range(OWN)]


def channel_at(chip, own):
    return (chip * OWN + own) * FILTERS


def part_at(chip):
    return slice(chip * FILTERS, (chip + 1) * FILTERS)


def stand(columns_ref, small_ref, taps_ref, skip_ref):
    small_ref[...] = jnp.zeros(small_ref.shape, f32)
    for branch in range(3):
        small_ref[8 * branch : 8 * branch + TAPS, :CHANNELS] = taps_ref[branch]
    small_ref[24:25, :CHANNELS] = skip_ref[...]
    columns_ref[...] = small_ref[...].T


def filtered(branch_ref, columns, branch, rows):
    lane = lax.broadcasted_iota(jnp.int32, (STEP, LANES), 1)
    taps = [jnp.broadcast_to(columns[:, 8 * branch + tap : 8 * branch + tap + 1], (STEP, LANES)) for tap in range(TAPS)]
    before = [jnp.zeros((STEP, LANES), f32)] * REACH
    for block in range(BLOCKS):
        own = branch_ref[branch, rows, block * LANES : (block + 1) * LANES].astype(f32)
        total = taps[0] * own
        for tap in range(1, TAPS):
            turned = pltpu.roll(own, tap, 1)
            total += taps[tap] * jnp.where(lane < tap, before[tap - 1], turned)
            before[tap - 1] = turned
        yield total


def short_kernel(
    branch_ref, taps_ref, skip_ref, signal_ref, edge_ref, query_ref, direct_ref, rows_ref, edges_ref, small_ref, columns_ref
):
    stand(columns_ref, small_ref, taps_ref, skip_ref)
    first = lax.broadcasted_iota(jnp.int32, (STEP, LANES), 1) < REACH

    def body(index, carry):
        rows = pl.ds(pl.multiple_of(index * STEP, STEP), STEP)
        columns = columns_ref[rows, :]
        skip = jnp.broadcast_to(columns[:, 24:25], (STEP, LANES))
        for block, total in enumerate(filtered(branch_ref, columns, 1, rows)):
            direct_ref[rows, block * LANES : (block + 1) * LANES] = total
            if block == 0:
                edges_ref[1, rows, :] = total
        for block, total in enumerate(filtered(branch_ref, columns, 2, rows)):
            at = slice(block * LANES, (block + 1) * LANES)
            gated = direct_ref[rows, at] * total
            direct_ref[rows, at] = skip * gated
            rows_ref[pl.ds(index * (STEP * BLOCKS) + block, STEP, stride=BLOCKS), :] = gated
            if block == 0:
                edges_ref[2, rows, :] = total
        for block, total in enumerate(filtered(branch_ref, columns, 0, rows)):
            at = slice(block * LANES, (block + 1) * LANES)
            direct = total * direct_ref[rows, at]
            query_ref[rows, at] = total if block else jnp.where(first, 1.0, total)
            direct_ref[rows, at] = direct if block else jnp.where(first, 0.0, direct)
            if block == 0:
                edges_ref[0, rows, :] = total
        return carry

    lax.fori_loop(0, CHANNELS // STEP, body, 0)
    for chip, own in PLACES:
        rows = rows_ref[channel_at(chip, own) * BLOCKS : (channel_at(chip, own) + FILTERS) * BLOCKS, :]
        signal_ref[part_at(chip), own * BLOCKS : (own + 1) * BLOCKS, :] = rows.reshape(FILTERS, BLOCKS, LANES).astype(bf16)
    lane = lax.broadcasted_iota(jnp.int32, (CHANNELS, LANES), 1)
    edge = jnp.where(lane < REACH, edges_ref[0], 0.0)
    for branch in range(3):
        if branch:
            edge += pltpu.roll(jnp.where(lane < REACH, edges_ref[branch], 0.0), 8 * branch, 1)
        place = 24 + 8 * branch
        last = branch_ref[branch, :, TOKENS - LANES :].astype(f32)
        for tap in range(1, TAPS):
            weight = columns_ref[:CHANNELS, 8 * branch + tap : 8 * branch + tap + 1]
            share = weight * pltpu.roll(last, place + tap, 1)
            edge += jnp.where((lane >= place) & (lane < place + tap), share, 0.0)
    skip = columns_ref[:CHANNELS, 24:25]
    high = edge.astype(bf16).astype(f32)
    skip_high = skip.astype(bf16).astype(f32)
    gains = jnp.where(lane < SKIP, 0.0, jnp.where(lane < SKIP + 8, skip_high, skip - skip_high))
    edges_ref[0] = high + pltpu.roll(edge - high, LOW, 1) + gains
    rows_ref[: PARTS * EDGE, :] = jnp.zeros((PARTS * EDGE, LANES), f32)
    for chip, own in PLACES:
        begin = channel_at(chip, own)
        rows_ref[pl.ds(chip * FILTERS * EDGE + own, FILTERS, stride=EDGE), :] = edges_ref[0, begin : begin + FILTERS, :]
    edge_ref[...] = rows_ref[: PARTS * EDGE, :].reshape(PARTS, EDGE, LANES).astype(bf16)


def pack_kernel(signal_ref, edge_ref, own_ref, other_ref, send_ref):
    send_ref[:, :HALF, :] = signal_ref[...]
    send_ref[:, EDGES_AT:, :] = edge_ref[...]
    chip = lax.div(lax.axis_index("ch"), 2)
    for at, taps_ref in ((chip, own_ref), (1 - chip, other_ref)):
        begin = pl.multiple_of(at * FILTERS, FILTERS)
        send_ref[pl.ds(begin, FILTERS), HALF:EDGES_AT, :] = taps_ref[...]


def conv_kernel(data_ref, *rest):
    *inputs, out_ref, signal_ref, taps_ref, edge_ref, left_ref, even_ref, odd_ref, sum_ref = rest
    core = lax.rem(lax.axis_index("ch"), 2)
    channel = 1 - core if inputs else core
    shift = 2 * GROUP
    groups = ROWS // shift
    row = lax.broadcasted_iota(jnp.int32, (WIDTH, LANES), 0)
    lane = lax.broadcasted_iota(jnp.int32, (WIDTH, LANES), 1)
    above = lane >= row
    low = lax.broadcasted_iota(jnp.int32, (ROWS, LANES), 1) < WIDTH
    right = (even_ref, odd_ref)
    previous = jnp.zeros((WIDTH, LANES), bf16)
    first = lax.broadcasted_iota(jnp.int32, (PARTS, LANES), 1) < REACH
    start = lax.broadcasted_iota(jnp.int32, (PARTS, LANES), 0) == 0
    edge_ref[...] = data_ref[:, EDGES_AT:, :].reshape(PARTS * EDGE, LANES).astype(f32)
    opening = pl.ds(shift, PARTS, stride=BLOCKS)

    def turn_back(value, by):
        return pltpu.roll(value, LANES - by, 1)

    def place(at):
        return pl.ds(pl.multiple_of(at * BLOCKS, BLOCKS), BLOCKS)

    def edges():
        rows = [edge_ref[pl.ds(at, PARTS, stride=EDGE), :] for at in range(OWN)]
        row = jnp.where(channel == 1, rows[1], rows[0])
        share = row + turn_back(row, LOW)
        other = jnp.where(start, 0.0, pltpu.roll(turn_back(share, 24), 1, 0))
        short = share + other
        gain = turn_back(row, SKIP) + turn_back(row, SKIP + 8)
        return short, turn_back(short, 8) * turn_back(short, 16), gain

    signal_ref[:shift, :] = jnp.zeros((shift, LANES), f32)
    signal_ref[shift:, :] = data_ref[:, place(channel), :].reshape(ROWS, LANES).astype(f32)
    signal_ref[opening, :] = jnp.where(first, edges()[1], signal_ref[opening, :])
    taps = inputs[0][...] if inputs else data_ref[:, HALF:EDGES_AT, :]
    taps_ref[...] = taps.reshape(ROWS, LANES).astype(f32)
    for lag in range(0, GROUP, 2):
        near = signal_ref[shift - 2 * lag : shift - 2 * lag + ROWS, :]
        far = signal_ref[shift - 2 * lag - 2 : shift - 2 * lag - 2 + ROWS, :]
        columns = slice(lag * WIDTH, (lag + 2) * WIDTH)
        left_ref[0, :, columns] = jnp.where(low, near, pltpu.roll(far, WIDTH, 1)).astype(bf16)
        left_ref[1, :, columns] = jnp.where(low, pltpu.roll(near, WIDTH, 1), far).astype(bf16)

    def toeplitz(group, lag, previous):
        block = group * shift + lag
        current = jnp.broadcast_to(taps_ref[block : block + 1, :], (WIDTH, LANES))
        current = pltpu.roll(current, 0, 1, stride=1, stride_axis=0).astype(bf16)
        right[group % 2][
            (lag // 2) * WIDTH : (lag // 2 + 1) * WIDTH, (lag % 2) * LANES : (lag % 2 + 1) * LANES
        ] = jnp.where(above, current, previous)
        return current

    for lag in range(shift):
        previous = toeplitz(0, lag, previous)
    for group in range(groups):
        for half in range(2):
            if group + 1 < groups:
                for lag in range(half * GROUP, (half + 1) * GROUP):
                    previous = toeplitz(group + 1, lag, previous)
            product = jnp.dot(
                left_ref[half, : ROWS - shift * group, :], right[group % 2][...], preferred_element_type=f32
            )
            if group == 0:
                sum_ref[half, shift:, :] = product
            else:
                sum_ref[half, shift + shift * group :, :] += product

    for half in range(2):
        sum_ref[half, :shift, :] = jnp.zeros((shift, 2 * LANES), f32)

    def gather(half, back):
        here, there = shift - back, shift - back - 1
        return sum_ref[half, here : here + ROWS, :LANES] + sum_ref[half, there : there + ROWS, LANES:]

    turned = jnp.where(low, pltpu.roll(gather(1, 1), WIDTH, 1), pltpu.roll(gather(1, 0), WIDTH, 1))
    signal_ref[shift:, :] = gather(0, 0) + turned
    query, gated, gain = edges()
    conv = signal_ref[opening, :]
    signal_ref[opening, :] = jnp.where(first, query * (conv + gain * gated), conv)
    result = signal_ref[shift:, :].astype(bf16).reshape(PARTS, BLOCKS, LANES)
    if inputs:
        out_ref[:, place(channel), :] = result
        out_ref[:, place(1 - channel), :] = inputs[1][...]
    else:
        out_ref[...] = result


def convolve(data, *inputs):
    return pl.pallas_call(
        conv_kernel,
        out_shape=jax.ShapeDtypeStruct((PARTS, HALF if inputs else BLOCKS, LANES), bf16),
        in_specs=[VMEM] * (1 + len(inputs)),
        out_specs=VMEM,
        scratch_shapes=[
            pltpu.VMEM((2 * GROUP + ROWS, LANES), f32),
            pltpu.VMEM((ROWS, LANES), f32),
            pltpu.VMEM((PARTS * EDGE, LANES), f32),
            pltpu.VMEM((2, ROWS, GROUP * WIDTH), bf16),
            pltpu.VMEM((GROUP * WIDTH, 2 * LANES), bf16),
            pltpu.VMEM((GROUP * WIDTH, 2 * LANES), bf16),
            pltpu.VMEM((2, 2 * GROUP + ROWS, 2 * LANES), f32),
        ],
        compiler_params=pltpu.CompilerParams(vmem_limit_bytes=16 * 2**20),
        cost_estimate=pl.CostEstimate(flops=4 * 10**9, bytes_accessed=2**20, transcendentals=0),
    )(data, *inputs)


def mix_kernel(conv_ref, query_ref, direct_ref, out_ref, rows_ref):
    for chip, own in PLACES:
        rows = conv_ref[part_at(chip), own * BLOCKS : (own + 1) * BLOCKS, :].reshape(FILTERS * BLOCKS, LANES)
        rows_ref[channel_at(chip, own) * BLOCKS : (channel_at(chip, own) + FILTERS) * BLOCKS, :] = rows.astype(f32)
    for block in range(BLOCKS):
        at = slice(block * LANES, (block + 1) * LANES)
        conv = rows_ref[pl.ds(block, CHANNELS, stride=BLOCKS), :]
        out_ref[:, at] = (query_ref[:, at] * conv + direct_ref[:, at]).astype(bf16)


def in_hbm(array):
    return pltpu.with_memory_space_constraint(array, pltpu.HBM)


def on_device(branches, short_taps, long_filter, skip_gain):
    own_filters, taps, skip, branches = pl.pallas_call(
        prepare_kernel,
        out_shape=[
            jax.ShapeDtypeStruct((FILTERS, BLOCKS, LANES), bf16),
            jax.ShapeDtypeStruct((3, TAPS, CHANNELS), f32),
            jax.ShapeDtypeStruct((1, CHANNELS), f32),
            jax.ShapeDtypeStruct((3, CHANNELS, TOKENS), bf16),
        ],
        in_specs=[pl.BlockSpec(memory_space=pltpu.HBM)] * 4,
        out_specs=[VMEM] * 4,
        scratch_shapes=[
            pltpu.VMEM((FILTERS, TOKENS), f32),
            pltpu.VMEM((FILTERS * BLOCKS, LANES), f32),
            pltpu.SemaphoreType.DMA((6,)),
        ],
        compiler_params=pltpu.CompilerParams(vmem_limit_bytes=8 * 2**20),
    )(in_hbm(long_filter), in_hbm(short_taps.transpose(0, 2, 1)), in_hbm(skip_gain[None, :]), in_hbm(branches))
    other_filters = lax.ppermute(own_filters, "ch", [(i, i ^ 2) for i in range(4)])
    signal, edge, query, direct = pl.pallas_call(
        short_kernel,
        out_shape=[
            jax.ShapeDtypeStruct((PARTS, HALF, LANES), bf16),
            jax.ShapeDtypeStruct((PARTS, EDGE, LANES), bf16),
            jax.ShapeDtypeStruct((CHANNELS, TOKENS), f32),
            jax.ShapeDtypeStruct((CHANNELS, TOKENS), f32),
        ],
        in_specs=[VMEM] * 3,
        out_specs=[VMEM] * 4,
        scratch_shapes=[
            pltpu.VMEM((CHANNELS * BLOCKS, LANES), f32),
            pltpu.VMEM((3, CHANNELS, LANES), f32),
            pltpu.VMEM((LANES, LANES), f32),
            pltpu.VMEM((LANES, LANES), f32),
        ],
        compiler_params=pltpu.CompilerParams(vmem_limit_bytes=16 * 2**20),
        cost_estimate=pl.CostEstimate(flops=10**7, bytes_accessed=8 * 2**20, transcendentals=0),
    )(branches, taps, skip)
    send = pl.pallas_call(
        pack_kernel,
        out_shape=jax.ShapeDtypeStruct((PARTS, EDGES_AT + EDGE, LANES), bf16),
        in_specs=[VMEM] * 4,
        out_specs=VMEM,
        compiler_params=pltpu.CompilerParams(vmem_limit_bytes=16 * 2**20),
    )(signal, edge, own_filters, other_filters)
    data = lax.all_to_all(send, "ctx", 0, 0, tiled=True)
    swapped = lax.ppermute(data[:, HALF:EDGES_AT, :], "ch", [(i, i ^ 1) for i in range(4)])
    conv = convolve(data, swapped, convolve(data))
    conv = lax.all_to_all(conv, "ctx", 0, 0, tiled=True)
    return pl.pallas_call(
        mix_kernel,
        out_shape=jax.ShapeDtypeStruct((CHANNELS, TOKENS), bf16),
        in_specs=[VMEM] * 3,
        out_specs=VMEM,
        scratch_shapes=[pltpu.VMEM((CHANNELS * BLOCKS, LANES), f32)],
        compiler_params=pltpu.CompilerParams(vmem_limit_bytes=32 * 2**20),
    )(conv, query, direct)


def solution(mesh):
    placed = (P(None, "ch", "ctx"), P(None, "ch", None), P("ch", "ctx"), P("ch"))
    return jax.shard_map(
        on_device, mesh=mesh, in_specs=placed, out_specs=P("ch", "ctx"), check_vma=False
    )
```

```python
import jax
import jax.numpy as jnp
from jax import lax
from jax.experimental import pallas as pl
from jax.experimental.pallas import tpu as pltpu
from jax.sharding import PartitionSpec as P

f32, bf16 = jnp.float32, jnp.bfloat16
LANES = 128
TAPS = 7
REACH = TAPS - 1
CHANNELS = 64
TOKENS = 2048
BLOCKS = TOKENS // LANES
PARTS = 32
FILTERS = 16
OWN = CHANNELS // PARTS
ROWS = PARTS * BLOCKS
HALF = OWN * BLOCKS
EDGES_AT = HALF + BLOCKS
EDGE = 8
LOW, SKIP = 48, 96
STEP = 16
GROUP = 8
WIDTH = LANES // 2
VMEM = pl.BlockSpec(memory_space=pltpu.VMEM)


def prepare_kernel(
    all_filters_ref, all_taps_ref, all_skip_ref, all_branches_ref, cast_ref, taps_ref, skip_ref, branches_ref,
    filters_ref, rows_ref, semaphores,
):
    sources = [all_filters_ref, all_taps_ref, all_skip_ref] + [all_branches_ref.at[branch] for branch in range(3)]
    targets = [filters_ref, taps_ref, skip_ref] + [branches_ref.at[branch] for branch in range(3)]
    copies = [
        pltpu.make_async_copy(source, target, semaphores.at[at])
        for at, (source, target) in enumerate(zip(sources, targets))
    ]
    for copy in copies:
        copy.start()
    copies[0].wait()
    for block in range(BLOCKS):
        rows_ref[pl.ds(block, FILTERS, stride=BLOCKS), :] = filters_ref[:, block * LANES : (block + 1) * LANES]
    cast_ref[...] = rows_ref[: FILTERS * BLOCKS, :].reshape(FILTERS, BLOCKS, LANES).astype(bf16)
    for copy in copies[1:]:
        copy.wait()


PLACES = [(chip, own) for chip in range(2) for own in range(OWN)]


def channel_at(chip, own):
    return (chip * OWN + own) * FILTERS


def part_at(chip):
    return slice(chip * FILTERS, (chip + 1) * FILTERS)


def stand(columns_ref, small_ref, taps_ref, skip_ref):
    small_ref[...] = jnp.zeros(small_ref.shape, f32)
    for branch in range(3):
        small_ref[8 * branch : 8 * branch + TAPS, :CHANNELS] = taps_ref[branch]
    small_ref[24:25, :CHANNELS] = skip_ref[...]
    columns_ref[...] = small_ref[...].T


def filtered(branch_ref, columns, branch, rows):
    lane = lax.broadcasted_iota(jnp.int32, (STEP, LANES), 1)
    taps = [jnp.broadcast_to(columns[:, 8 * branch + tap : 8 * branch + tap + 1], (STEP, LANES)) for tap in range(TAPS)]
    before = [jnp.zeros((STEP, LANES), f32)] * REACH
    for block in range(BLOCKS):
        own = branch_ref[branch, rows, block * LANES : (block + 1) * LANES].astype(f32)
        total = taps[0] * own
        for tap in range(1, TAPS):
            turned = pltpu.roll(own, tap, 1)
            total += taps[tap] * jnp.where(lane < tap, before[tap - 1], turned)
            before[tap - 1] = turned
        yield total


def short_kernel(
    branch_ref, taps_ref, skip_ref, signal_ref, edge_ref, query_ref, direct_ref, rows_ref, edges_ref, small_ref, columns_ref
):
    stand(columns_ref, small_ref, taps_ref, skip_ref)
    first = lax.broadcasted_iota(jnp.int32, (STEP, LANES), 1) < REACH

    def body(index, carry):
        rows = pl.ds(pl.multiple_of(index * STEP, STEP), STEP)
        columns = columns_ref[rows, :]
        skip = jnp.broadcast_to(columns[:, 24:25], (STEP, LANES))
        for block, total in enumerate(filtered(branch_ref, columns, 1, rows)):
            direct_ref[rows, block * LANES : (block + 1) * LANES] = total
            if block == 0:
                edges_ref[1, rows, :] = total
        for block, total in enumerate(filtered(branch_ref, columns, 2, rows)):
            at = slice(block * LANES, (block + 1) * LANES)
            gated = direct_ref[rows, at] * total
            direct_ref[rows, at] = skip * gated
            rows_ref[pl.ds(index * (STEP * BLOCKS) + block, STEP, stride=BLOCKS), :] = gated
            if block == 0:
                edges_ref[2, rows, :] = total
        for block, total in enumerate(filtered(branch_ref, columns, 0, rows)):
            at = slice(block * LANES, (block + 1) * LANES)
            direct = total * direct_ref[rows, at]
            query_ref[rows, at] = total if block else jnp.where(first, 1.0, total)
            direct_ref[rows, at] = direct if block else jnp.where(first, 0.0, direct)
            if block == 0:
                edges_ref[0, rows, :] = total
        return carry

    lax.fori_loop(0, CHANNELS // STEP, body, 0)
    for chip, own in PLACES:
        rows = rows_ref[channel_at(chip, own) * BLOCKS : (channel_at(chip, own) + FILTERS) * BLOCKS, :]
        signal_ref[part_at(chip), own * BLOCKS : (own + 1) * BLOCKS, :] = rows.reshape(FILTERS, BLOCKS, LANES).astype(bf16)
    lane = lax.broadcasted_iota(jnp.int32, (CHANNELS, LANES), 1)
    edge = jnp.where(lane < REACH, edges_ref[0], 0.0)
    for branch in range(3):
        if branch:
            edge += pltpu.roll(jnp.where(lane < REACH, edges_ref[branch], 0.0), 8 * branch, 1)
        place = 24 + 8 * branch
        last = branch_ref[branch, :, TOKENS - LANES :].astype(f32)
        for tap in range(1, TAPS):
            weight = columns_ref[:CHANNELS, 8 * branch + tap : 8 * branch + tap + 1]
            share = weight * pltpu.roll(last, place + tap, 1)
            edge += jnp.where((lane >= place) & (lane < place + tap), share, 0.0)
    skip = columns_ref[:CHANNELS, 24:25]
    high = edge.astype(bf16).astype(f32)
    skip_high = skip.astype(bf16).astype(f32)
    gains = jnp.where(lane < SKIP, 0.0, jnp.where(lane < SKIP + 8, skip_high, skip - skip_high))
    edges_ref[0] = high + pltpu.roll(edge - high, LOW, 1) + gains
    rows_ref[: PARTS * EDGE, :] = jnp.zeros((PARTS * EDGE, LANES), f32)
    for chip, own in PLACES:
        begin = channel_at(chip, own)
        rows_ref[pl.ds(chip * FILTERS * EDGE + own, FILTERS, stride=EDGE), :] = edges_ref[0, begin : begin + FILTERS, :]
    edge_ref[...] = rows_ref[: PARTS * EDGE, :].reshape(PARTS, EDGE, LANES).astype(bf16)


def pack_kernel(signal_ref, edge_ref, own_ref, other_ref, send_ref):
    send_ref[:, :HALF, :] = signal_ref[...]
    send_ref[:, EDGES_AT:, :] = edge_ref[...]
    chip = lax.div(lax.axis_index("ch"), 2)
    for at, taps_ref in ((chip, own_ref), (1 - chip, other_ref)):
        begin = pl.multiple_of(at * FILTERS, FILTERS)
        send_ref[pl.ds(begin, FILTERS), HALF:EDGES_AT, :] = taps_ref[...]


def conv_kernel(data_ref, *rest):
    *inputs, out_ref, signal_ref, taps_ref, edge_ref, left_ref, even_ref, odd_ref, sum_ref = rest
    core = lax.rem(lax.axis_index("ch"), 2)
    channel = 1 - core if inputs else core
    shift = 2 * GROUP
    groups = ROWS // shift
    row = lax.broadcasted_iota(jnp.int32, (WIDTH, LANES), 0)
    lane = lax.broadcasted_iota(jnp.int32, (WIDTH, LANES), 1)
    above = lane >= row
    low = lax.broadcasted_iota(jnp.int32, (ROWS, LANES), 1) < WIDTH
    right = (even_ref, odd_ref)
    previous = jnp.zeros((WIDTH, LANES), bf16)
    first = lax.broadcasted_iota(jnp.int32, (PARTS, LANES), 1) < REACH
    start = lax.broadcasted_iota(jnp.int32, (PARTS, LANES), 0) == 0
    edge_ref[: PARTS * EDGE, :] = data_ref[:, EDGES_AT:, :].reshape(PARTS * EDGE, LANES).astype(f32)
    opening = pl.ds(shift, PARTS, stride=BLOCKS)

    def turn_back(value, by):
        return pltpu.roll(value, LANES - by, 1)

    def place(at):
        return pl.ds(pl.multiple_of(at * BLOCKS, BLOCKS), BLOCKS)

    def edges():
        rows = [edge_ref[pl.ds(at, PARTS, stride=EDGE), :] for at in range(OWN)]
        row = jnp.where(channel == 1, rows[1], rows[0])
        share = row + turn_back(row, LOW)
        other = jnp.where(start, 0.0, pltpu.roll(turn_back(share, 24), 1, 0))
        short = share + other
        gain = turn_back(row, SKIP) + turn_back(row, SKIP + 8)
        return short, turn_back(short, 8) * turn_back(short, 16), gain

    signal_ref[:shift, :] = jnp.zeros((shift, LANES), f32)
    signal_ref[shift:, :] = data_ref[:, place(channel), :].reshape(ROWS, LANES).astype(f32)
    signal_ref[opening, :] = jnp.where(first, edges()[1], signal_ref[opening, :])
    taps = inputs[0][...] if inputs else data_ref[:, HALF:EDGES_AT, :]
    taps_ref[...] = taps.reshape(ROWS, LANES).astype(f32)
    for lag in range(0, GROUP, 2):
        near = signal_ref[shift - 2 * lag : shift - 2 * lag + ROWS, :]
        far = signal_ref[shift - 2 * lag - 2 : shift - 2 * lag - 2 + ROWS, :]
        columns = slice(lag * WIDTH, (lag + 2) * WIDTH)
        left_ref[0, :, columns] = jnp.where(low, near, pltpu.roll(far, WIDTH, 1)).astype(bf16)
        left_ref[1, :, columns] = jnp.where(low, pltpu.roll(near, WIDTH, 1), far).astype(bf16)

    def toeplitz(group, lag, previous):
        block = group * shift + lag
        current = jnp.broadcast_to(taps_ref[block : block + 1, :], (WIDTH, LANES))
        current = pltpu.roll(current, 0, 1, stride=1, stride_axis=0).astype(bf16)
        right[group % 2][
            (lag // 2) * WIDTH : (lag // 2 + 1) * WIDTH, (lag % 2) * LANES : (lag % 2 + 1) * LANES
        ] = jnp.where(above, current, previous)
        return current

    for lag in range(shift):
        previous = toeplitz(0, lag, previous)
    for group in range(groups):
        for half in range(2):
            if group + 1 < groups:
                for lag in range(half * GROUP, (half + 1) * GROUP):
                    previous = toeplitz(group + 1, lag, previous)
            product = jnp.dot(
                left_ref[half, : ROWS - shift * group, :], right[group % 2][...], preferred_element_type=f32
            )
            if group == 0:
                sum_ref[half, shift:, :] = product
            else:
                sum_ref[half, shift + shift * group :, :] += product

    for half in range(2):
        sum_ref[half, :shift, :] = jnp.zeros((shift, 2 * LANES), f32)

    def gather(half, back):
        here, there = shift - back, shift - back - 1
        return sum_ref[half, here : here + ROWS, :LANES] + sum_ref[half, there : there + ROWS, LANES:]

    turned = jnp.where(low, pltpu.roll(gather(1, 1), WIDTH, 1), pltpu.roll(gather(1, 0), WIDTH, 1))
    signal_ref[shift:, :] = gather(0, 0) + turned
    query, gated, gain = edges()
    conv = signal_ref[opening, :]
    signal_ref[opening, :] = jnp.where(first, query * (conv + gain * gated), conv)
    result = signal_ref[shift:, :].astype(bf16).reshape(PARTS, BLOCKS, LANES)
    if inputs:
        out_ref[:, place(channel), :] = result
        out_ref[:, place(1 - channel), :] = inputs[1][...]
    else:
        out_ref[...] = result


def convolve(data, *inputs):
    return pl.pallas_call(
        conv_kernel,
        out_shape=jax.ShapeDtypeStruct((PARTS, HALF if inputs else BLOCKS, LANES), bf16),
        in_specs=[VMEM] * (1 + len(inputs)),
        out_specs=VMEM,
        scratch_shapes=[
            pltpu.VMEM((2 * GROUP + ROWS, LANES), f32),
            pltpu.VMEM((ROWS, LANES), f32),
            pltpu.VMEM((PARTS * EDGE + EDGE, LANES), f32),
            pltpu.VMEM((2, ROWS, GROUP * WIDTH), bf16),
            pltpu.VMEM((GROUP * WIDTH, 2 * LANES), bf16),
            pltpu.VMEM((GROUP * WIDTH, 2 * LANES), bf16),
            pltpu.VMEM((2, 2 * GROUP + ROWS, 2 * LANES), f32),
        ],
        compiler_params=pltpu.CompilerParams(vmem_limit_bytes=16 * 2**20),
        cost_estimate=pl.CostEstimate(flops=4 * 10**9, bytes_accessed=2**20, transcendentals=0),
    )(data, *inputs)


def mix_kernel(conv_ref, query_ref, direct_ref, out_ref, rows_ref, mixed_ref, semaphores):
    copies = []
    for chip, own in PLACES:
        begin = channel_at(chip, own)
        channels = slice(begin, begin + FILTERS)
        rows = conv_ref[part_at(chip), own * BLOCKS : (own + 1) * BLOCKS, :].reshape(FILTERS * BLOCKS, LANES)
        rows_ref[begin * BLOCKS : (begin + FILTERS) * BLOCKS, :] = rows.astype(f32)
        for block in range(BLOCKS):
            at = slice(block * LANES, (block + 1) * LANES)
            conv = rows_ref[pl.ds(begin * BLOCKS + block, FILTERS, stride=BLOCKS), :]
            mixed_ref[channels, at] = (query_ref[channels, at] * conv + direct_ref[channels, at]).astype(bf16)
        slot = len(copies)
        copies.append(pltpu.make_async_copy(mixed_ref.at[channels, :], out_ref.at[channels, :], semaphores.at[slot]))
        copies[-1].start()
    for copy in copies:
        copy.wait()


def in_hbm(array):
    return pltpu.with_memory_space_constraint(array, pltpu.HBM)


def on_device(branches, short_taps, long_filter, skip_gain):
    own_filters, taps, skip, branches = pl.pallas_call(
        prepare_kernel,
        out_shape=[
            jax.ShapeDtypeStruct((FILTERS, BLOCKS, LANES), bf16),
            jax.ShapeDtypeStruct((3, TAPS, CHANNELS), f32),
            jax.ShapeDtypeStruct((1, CHANNELS), f32),
            jax.ShapeDtypeStruct((3, CHANNELS, TOKENS), bf16),
        ],
        in_specs=[pl.BlockSpec(memory_space=pltpu.HBM)] * 4,
        out_specs=[VMEM] * 4,
        scratch_shapes=[
            pltpu.VMEM((FILTERS, TOKENS), f32),
            pltpu.VMEM((FILTERS * BLOCKS + BLOCKS, LANES), f32),
            pltpu.SemaphoreType.DMA((6,)),
        ],
        compiler_params=pltpu.CompilerParams(vmem_limit_bytes=8 * 2**20),
    )(in_hbm(long_filter), in_hbm(short_taps.transpose(0, 2, 1)), in_hbm(skip_gain[None, :]), in_hbm(branches))
    other_filters = lax.ppermute(own_filters, "ch", [(i, i ^ 2) for i in range(4)])
    signal, edge, query, direct = pl.pallas_call(
        short_kernel,
        out_shape=[
            jax.ShapeDtypeStruct((PARTS, HALF, LANES), bf16),
            jax.ShapeDtypeStruct((PARTS, EDGE, LANES), bf16),
            jax.ShapeDtypeStruct((CHANNELS, TOKENS), f32),
            jax.ShapeDtypeStruct((CHANNELS, TOKENS), f32),
        ],
        in_specs=[VMEM] * 3,
        out_specs=[VMEM] * 4,
        scratch_shapes=[
            pltpu.VMEM((CHANNELS * BLOCKS + BLOCKS, LANES), f32),
            pltpu.VMEM((3, CHANNELS, LANES), f32),
            pltpu.VMEM((LANES, LANES), f32),
            pltpu.VMEM((LANES, LANES), f32),
        ],
        compiler_params=pltpu.CompilerParams(vmem_limit_bytes=16 * 2**20),
        cost_estimate=pl.CostEstimate(flops=10**7, bytes_accessed=8 * 2**20, transcendentals=0),
    )(branches, taps, skip)
    send = pl.pallas_call(
        pack_kernel,
        out_shape=jax.ShapeDtypeStruct((PARTS, EDGES_AT + EDGE, LANES), bf16),
        in_specs=[VMEM] * 4,
        out_specs=VMEM,
        compiler_params=pltpu.CompilerParams(vmem_limit_bytes=16 * 2**20),
    )(signal, edge, own_filters, other_filters)
    data = lax.all_to_all(send, "ctx", 0, 0, tiled=True)
    swapped = lax.ppermute(data[:, HALF:EDGES_AT, :], "ch", [(i, i ^ 1) for i in range(4)])
    conv = convolve(data, swapped, convolve(data))
    conv = lax.all_to_all(conv, "ctx", 0, 0, tiled=True)
    return pl.pallas_call(
        mix_kernel,
        out_shape=jax.ShapeDtypeStruct((CHANNELS, TOKENS), bf16),
        in_specs=[VMEM] * 3,
        out_specs=pl.BlockSpec(memory_space=pltpu.HBM),
        scratch_shapes=[
            pltpu.VMEM((CHANNELS * BLOCKS + BLOCKS, LANES), f32),
            pltpu.VMEM((CHANNELS, TOKENS), bf16),
            pltpu.SemaphoreType.DMA((len(PLACES),)),
        ],
        compiler_params=pltpu.CompilerParams(vmem_limit_bytes=32 * 2**20),
    )(conv, query, direct)


def solution(mesh):
    placed = (P(None, "ch", "ctx"), P(None, "ch", None), P("ch", "ctx"), P("ch"))
    return jax.shard_map(
        on_device, mesh=mesh, in_specs=placed, out_specs=P("ch", "ctx"), check_vma=False
    )
```

```python
import jax
import jax.numpy as jnp
from jax import lax
from jax.experimental import pallas as pl
from jax.experimental.pallas import tpu as pltpu
from jax.sharding import PartitionSpec as P

f32, bf16 = jnp.float32, jnp.bfloat16
LANES = 128
TAPS = 7
REACH = TAPS - 1
CHANNELS = 64
TOKENS = 2048
BLOCKS = TOKENS // LANES
PARTS = 32
FILTERS = 16
OWN = CHANNELS // PARTS
ROWS = PARTS * BLOCKS
HALF = OWN * BLOCKS
EDGES_AT = HALF + BLOCKS
EDGE = 8
LOW, SKIP = 48, 96
STEP = 16
GROUP = 8
WIDTH = LANES // 2
VMEM = pl.BlockSpec(memory_space=pltpu.VMEM)


def prepare_kernel(
    all_filters_ref, all_taps_ref, all_skip_ref, all_branches_ref, cast_ref, columns_ref, branches_ref,
    filters_ref, taps_ref, skip_ref, small_ref, rows_ref, semaphores,
):
    sources = [all_filters_ref, all_taps_ref, all_skip_ref] + [all_branches_ref.at[branch] for branch in range(3)]
    targets = [filters_ref, taps_ref, skip_ref] + [branches_ref.at[branch] for branch in range(3)]
    copies = [
        pltpu.make_async_copy(source, target, semaphores.at[at])
        for at, (source, target) in enumerate(zip(sources, targets))
    ]
    for copy in copies:
        copy.start()
    copies[0].wait()
    for block in range(BLOCKS):
        rows_ref[pl.ds(block, FILTERS, stride=BLOCKS), :] = filters_ref[:, block * LANES : (block + 1) * LANES]
    cast_ref[...] = rows_ref[: FILTERS * BLOCKS, :].reshape(FILTERS, BLOCKS, LANES).astype(bf16)
    for copy in copies[1:3]:
        copy.wait()
    stand(columns_ref, small_ref, taps_ref, skip_ref)
    for copy in copies[3:]:
        copy.wait()


PLACES = [(chip, own) for chip in range(2) for own in range(OWN)]


def channel_at(chip, own):
    return (chip * OWN + own) * FILTERS


def part_at(chip):
    return slice(chip * FILTERS, (chip + 1) * FILTERS)


def stand(columns_ref, small_ref, taps_ref, skip_ref):
    small_ref[...] = jnp.zeros(small_ref.shape, f32)
    for branch in range(3):
        small_ref[8 * branch : 8 * branch + TAPS, :CHANNELS] = taps_ref[branch]
    small_ref[24:25, :CHANNELS] = skip_ref[...]
    columns_ref[...] = small_ref[...].T


def filtered(branch_ref, columns, branch, rows):
    lane = lax.broadcasted_iota(jnp.int32, (STEP, LANES), 1)
    taps = [jnp.broadcast_to(columns[:, 8 * branch + tap : 8 * branch + tap + 1], (STEP, LANES)) for tap in range(TAPS)]
    before = [jnp.zeros((STEP, LANES), f32)] * REACH
    for block in range(BLOCKS):
        own = branch_ref[branch, rows, block * LANES : (block + 1) * LANES].astype(f32)
        total = taps[0] * own
        for tap in range(1, TAPS):
            turned = pltpu.roll(own, tap, 1)
            total += taps[tap] * jnp.where(lane < tap, before[tap - 1], turned)
            before[tap - 1] = turned
        yield total


def short_kernel(
    branch_ref, columns_ref, signal_ref, edge_ref, query_ref, direct_ref, rows_ref, edges_ref
):
    first = lax.broadcasted_iota(jnp.int32, (STEP, LANES), 1) < REACH

    def body(index, carry):
        rows = pl.ds(pl.multiple_of(index * STEP, STEP), STEP)
        columns = columns_ref[rows, :]
        skip = jnp.broadcast_to(columns[:, 24:25], (STEP, LANES))
        for block, total in enumerate(filtered(branch_ref, columns, 1, rows)):
            direct_ref[rows, block * LANES : (block + 1) * LANES] = total
            if block == 0:
                edges_ref[1, rows, :] = total
        for block, total in enumerate(filtered(branch_ref, columns, 2, rows)):
            at = slice(block * LANES, (block + 1) * LANES)
            gated = direct_ref[rows, at] * total
            direct_ref[rows, at] = skip * gated
            rows_ref[pl.ds(index * (STEP * BLOCKS) + block, STEP, stride=BLOCKS), :] = gated
            if block == 0:
                edges_ref[2, rows, :] = total
        for block, total in enumerate(filtered(branch_ref, columns, 0, rows)):
            at = slice(block * LANES, (block + 1) * LANES)
            direct = total * direct_ref[rows, at]
            query_ref[rows, at] = total if block else jnp.where(first, 1.0, total)
            direct_ref[rows, at] = direct if block else jnp.where(first, 0.0, direct)
            if block == 0:
                edges_ref[0, rows, :] = total
        return carry

    lax.fori_loop(0, CHANNELS // STEP, body, 0)
    for chip, own in PLACES:
        rows = rows_ref[channel_at(chip, own) * BLOCKS : (channel_at(chip, own) + FILTERS) * BLOCKS, :]
        signal_ref[part_at(chip), own * BLOCKS : (own + 1) * BLOCKS, :] = rows.reshape(FILTERS, BLOCKS, LANES).astype(bf16)
    lane = lax.broadcasted_iota(jnp.int32, (CHANNELS, LANES), 1)
    edge = jnp.where(lane < REACH, edges_ref[0], 0.0)
    for branch in range(3):
        if branch:
            edge += pltpu.roll(jnp.where(lane < REACH, edges_ref[branch], 0.0), 8 * branch, 1)
        place = 24 + 8 * branch
        last = branch_ref[branch, :, TOKENS - LANES :].astype(f32)
        for tap in range(1, TAPS):
            weight = columns_ref[:CHANNELS, 8 * branch + tap : 8 * branch + tap + 1]
            share = weight * pltpu.roll(last, place + tap, 1)
            edge += jnp.where((lane >= place) & (lane < place + tap), share, 0.0)
    skip = columns_ref[:CHANNELS, 24:25]
    high = edge.astype(bf16).astype(f32)
    skip_high = skip.astype(bf16).astype(f32)
    gains = jnp.where(lane < SKIP, 0.0, jnp.where(lane < SKIP + 8, skip_high, skip - skip_high))
    edges_ref[0] = high + pltpu.roll(edge - high, LOW, 1) + gains
    rows_ref[: PARTS * EDGE, :] = jnp.zeros((PARTS * EDGE, LANES), f32)
    for chip, own in PLACES:
        begin = channel_at(chip, own)
        rows_ref[pl.ds(chip * FILTERS * EDGE + own, FILTERS, stride=EDGE), :] = edges_ref[0, begin : begin + FILTERS, :]
    edge_ref[...] = rows_ref[: PARTS * EDGE, :].reshape(PARTS, EDGE, LANES).astype(bf16)


def pack_kernel(signal_ref, edge_ref, own_ref, other_ref, send_ref):
    send_ref[:, :HALF, :] = signal_ref[...]
    send_ref[:, EDGES_AT:, :] = edge_ref[...]
    chip = lax.div(lax.axis_index("ch"), 2)
    for at, taps_ref in ((chip, own_ref), (1 - chip, other_ref)):
        begin = pl.multiple_of(at * FILTERS, FILTERS)
        send_ref[pl.ds(begin, FILTERS), HALF:EDGES_AT, :] = taps_ref[...]


def conv_kernel(data_ref, *rest):
    *inputs, out_ref, signal_ref, taps_ref, edge_ref, left_ref, even_ref, odd_ref, sum_ref = rest
    core = lax.rem(lax.axis_index("ch"), 2)
    channel = 1 - core if inputs else core
    shift = 2 * GROUP
    groups = ROWS // shift
    row = lax.broadcasted_iota(jnp.int32, (WIDTH, LANES), 0)
    lane = lax.broadcasted_iota(jnp.int32, (WIDTH, LANES), 1)
    above = lane >= row
    low = lax.broadcasted_iota(jnp.int32, (ROWS, LANES), 1) < WIDTH
    right = (even_ref, odd_ref)
    previous = jnp.zeros((WIDTH, LANES), bf16)
    first = lax.broadcasted_iota(jnp.int32, (PARTS, LANES), 1) < REACH
    start = lax.broadcasted_iota(jnp.int32, (PARTS, LANES), 0) == 0
    edge_ref[: PARTS * EDGE, :] = data_ref[:, EDGES_AT:, :].reshape(PARTS * EDGE, LANES).astype(f32)
    opening = pl.ds(shift, PARTS, stride=BLOCKS)

    def turn_back(value, by):
        return pltpu.roll(value, LANES - by, 1)

    def place(at):
        return pl.ds(pl.multiple_of(at * BLOCKS, BLOCKS), BLOCKS)

    def edges():
        rows = [edge_ref[pl.ds(at, PARTS, stride=EDGE), :] for at in range(OWN)]
        row = jnp.where(channel == 1, rows[1], rows[0])
        share = row + turn_back(row, LOW)
        other = jnp.where(start, 0.0, pltpu.roll(turn_back(share, 24), 1, 0))
        short = share + other
        gain = turn_back(row, SKIP) + turn_back(row, SKIP + 8)
        return short, turn_back(short, 8) * turn_back(short, 16), gain

    signal_ref[:shift, :] = jnp.zeros((shift, LANES), f32)
    signal_ref[shift:, :] = data_ref[:, place(channel), :].reshape(ROWS, LANES).astype(f32)
    signal_ref[opening, :] = jnp.where(first, edges()[1], signal_ref[opening, :])
    taps = inputs[0][...] if inputs else data_ref[:, HALF:EDGES_AT, :]
    taps_ref[...] = taps.reshape(ROWS, LANES).astype(f32)
    for lag in range(0, GROUP, 2):
        near = signal_ref[shift - 2 * lag : shift - 2 * lag + ROWS, :]
        far = signal_ref[shift - 2 * lag - 2 : shift - 2 * lag - 2 + ROWS, :]
        columns = slice(lag * WIDTH, (lag + 2) * WIDTH)
        left_ref[0, :, columns] = jnp.where(low, near, pltpu.roll(far, WIDTH, 1)).astype(bf16)
        left_ref[1, :, columns] = jnp.where(low, pltpu.roll(near, WIDTH, 1), far).astype(bf16)

    def toeplitz(group, lag, previous):
        block = group * shift + lag
        current = jnp.broadcast_to(taps_ref[block : block + 1, :], (WIDTH, LANES))
        current = pltpu.roll(current, 0, 1, stride=1, stride_axis=0).astype(bf16)
        right[group % 2][
            (lag // 2) * WIDTH : (lag // 2 + 1) * WIDTH, (lag % 2) * LANES : (lag % 2 + 1) * LANES
        ] = jnp.where(above, current, previous)
        return current

    for lag in range(shift):
        previous = toeplitz(0, lag, previous)
    for group in range(groups):
        for half in range(2):
            if group + 1 < groups:
                for lag in range(half * GROUP, (half + 1) * GROUP):
                    previous = toeplitz(group + 1, lag, previous)
            product = jnp.dot(
                left_ref[half, : ROWS - shift * group, :], right[group % 2][...], preferred_element_type=f32
            )
            if group == 0:
                sum_ref[half, shift:, :] = product
            else:
                sum_ref[half, shift + shift * group :, :] += product

    for half in range(2):
        sum_ref[half, :shift, :] = jnp.zeros((shift, 2 * LANES), f32)

    def gather(half, back):
        here, there = shift - back, shift - back - 1
        return sum_ref[half, here : here + ROWS, :LANES] + sum_ref[half, there : there + ROWS, LANES:]

    turned = jnp.where(low, pltpu.roll(gather(1, 1), WIDTH, 1), pltpu.roll(gather(1, 0), WIDTH, 1))
    signal_ref[shift:, :] = gather(0, 0) + turned
    query, gated, gain = edges()
    conv = signal_ref[opening, :]
    signal_ref[opening, :] = jnp.where(first, query * (conv + gain * gated), conv)
    result = signal_ref[shift:, :].astype(bf16).reshape(PARTS, BLOCKS, LANES)
    if inputs:
        out_ref[:, place(channel), :] = result
        out_ref[:, place(1 - channel), :] = inputs[1][...]
    else:
        out_ref[...] = result


def convolve(data, *inputs):
    return pl.pallas_call(
        conv_kernel,
        out_shape=jax.ShapeDtypeStruct((PARTS, HALF if inputs else BLOCKS, LANES), bf16),
        in_specs=[VMEM] * (1 + len(inputs)),
        out_specs=VMEM,
        scratch_shapes=[
            pltpu.VMEM((2 * GROUP + ROWS, LANES), f32),
            pltpu.VMEM((ROWS, LANES), f32),
            pltpu.VMEM((PARTS * EDGE + EDGE, LANES), f32),
            pltpu.VMEM((2, ROWS, GROUP * WIDTH), bf16),
            pltpu.VMEM((GROUP * WIDTH, 2 * LANES), bf16),
            pltpu.VMEM((GROUP * WIDTH, 2 * LANES), bf16),
            pltpu.VMEM((2, 2 * GROUP + ROWS, 2 * LANES), f32),
        ],
        compiler_params=pltpu.CompilerParams(vmem_limit_bytes=16 * 2**20),
        cost_estimate=pl.CostEstimate(flops=4 * 10**9, bytes_accessed=2**20, transcendentals=0),
    )(data, *inputs)


def mix_kernel(conv_ref, query_ref, direct_ref, out_ref, rows_ref, mixed_ref, semaphores):
    copies = []
    for chip, own in PLACES:
        begin = channel_at(chip, own)
        channels = slice(begin, begin + FILTERS)
        rows = conv_ref[part_at(chip), own * BLOCKS : (own + 1) * BLOCKS, :].reshape(FILTERS * BLOCKS, LANES)
        rows_ref[begin * BLOCKS : (begin + FILTERS) * BLOCKS, :] = rows.astype(f32)
        for block in range(BLOCKS):
            at = slice(block * LANES, (block + 1) * LANES)
            conv = rows_ref[pl.ds(begin * BLOCKS + block, FILTERS, stride=BLOCKS), :]
            mixed_ref[channels, at] = (query_ref[channels, at] * conv + direct_ref[channels, at]).astype(bf16)
        slot = len(copies)
        copies.append(pltpu.make_async_copy(mixed_ref.at[channels, :], out_ref.at[channels, :], semaphores.at[slot]))
        copies[-1].start()
    for copy in copies:
        copy.wait()


def in_hbm(array):
    return pltpu.with_memory_space_constraint(array, pltpu.HBM)


def on_device(branches, short_taps, long_filter, skip_gain):
    own_filters, columns, branches = pl.pallas_call(
        prepare_kernel,
        out_shape=[
            jax.ShapeDtypeStruct((FILTERS, BLOCKS, LANES), bf16),
            jax.ShapeDtypeStruct((LANES, LANES), f32),
            jax.ShapeDtypeStruct((3, CHANNELS, TOKENS), bf16),
        ],
        in_specs=[pl.BlockSpec(memory_space=pltpu.HBM)] * 4,
        out_specs=[VMEM] * 3,
        scratch_shapes=[
            pltpu.VMEM((FILTERS, TOKENS), f32),
            pltpu.VMEM((3, TAPS, CHANNELS), f32),
            pltpu.VMEM((1, CHANNELS), f32),
            pltpu.VMEM((LANES, LANES), f32),
            pltpu.VMEM((FILTERS * BLOCKS + BLOCKS, LANES), f32),
            pltpu.SemaphoreType.DMA((6,)),
        ],
        compiler_params=pltpu.CompilerParams(vmem_limit_bytes=8 * 2**20),
    )(in_hbm(long_filter), in_hbm(short_taps.transpose(0, 2, 1)), in_hbm(skip_gain[None, :]), in_hbm(branches))
    other_filters = lax.ppermute(own_filters, "ch", [(i, i ^ 2) for i in range(4)])
    signal, edge, query, direct = pl.pallas_call(
        short_kernel,
        out_shape=[
            jax.ShapeDtypeStruct((PARTS, HALF, LANES), bf16),
            jax.ShapeDtypeStruct((PARTS, EDGE, LANES), bf16),
            jax.ShapeDtypeStruct((CHANNELS, TOKENS), f32),
            jax.ShapeDtypeStruct((CHANNELS, TOKENS), f32),
        ],
        in_specs=[VMEM] * 2,
        out_specs=[VMEM] * 4,
        scratch_shapes=[
            pltpu.VMEM((CHANNELS * BLOCKS + BLOCKS, LANES), f32),
            pltpu.VMEM((3, CHANNELS, LANES), f32),
        ],
        compiler_params=pltpu.CompilerParams(vmem_limit_bytes=16 * 2**20),
        cost_estimate=pl.CostEstimate(flops=10**7, bytes_accessed=8 * 2**20, transcendentals=0),
    )(branches, columns)
    send = pl.pallas_call(
        pack_kernel,
        out_shape=jax.ShapeDtypeStruct((PARTS, EDGES_AT + EDGE, LANES), bf16),
        in_specs=[VMEM] * 4,
        out_specs=VMEM,
        compiler_params=pltpu.CompilerParams(vmem_limit_bytes=16 * 2**20),
    )(signal, edge, own_filters, other_filters)
    data = lax.all_to_all(send, "ctx", 0, 0, tiled=True)
    swapped = lax.ppermute(data[:, HALF:EDGES_AT, :], "ch", [(i, i ^ 1) for i in range(4)])
    conv = convolve(data, swapped, convolve(data))
    conv = lax.all_to_all(conv, "ctx", 0, 0, tiled=True)
    return pl.pallas_call(
        mix_kernel,
        out_shape=jax.ShapeDtypeStruct((CHANNELS, TOKENS), bf16),
        in_specs=[VMEM] * 3,
        out_specs=pl.BlockSpec(memory_space=pltpu.HBM),
        scratch_shapes=[
            pltpu.VMEM((CHANNELS * BLOCKS + BLOCKS, LANES), f32),
            pltpu.VMEM((CHANNELS, TOKENS), bf16),
            pltpu.SemaphoreType.DMA((len(PLACES),)),
        ],
        compiler_params=pltpu.CompilerParams(vmem_limit_bytes=32 * 2**20),
    )(conv, query, direct)


def solution(mesh):
    placed = (P(None, "ch", "ctx"), P(None, "ch", None), P("ch", "ctx"), P("ch"))
    return jax.shard_map(
        on_device, mesh=mesh, in_specs=placed, out_specs=P("ch", "ctx"), check_vma=False
    )
```
